32 devices in a mesh: section: 4 (over y, x), dp: 8 (over z, core).
Axes of the slice: x: 2, y: 2, z: 4, core: 2. Of those that a mesh axis runs over, the one named last changes fastest.
Arguments:
- inputs: bfloat16 [2, 4096, 1024], P(None, 'dp'), may hold values from -6 to 6
- cotangent: bfloat16 [2, 4096, 1024], P(None, 'dp'), may hold values from -6 to 6
- seq_lengths: int32 [2, 8, 2], P(None, 'dp'), may hold values from 1 to 511, as said below
- flat_params: float32 [4, 8455168], P('section', 'dp'), may hold values from -8 to 8, as said below
Outputs:
- section_outputs: bfloat16 [4, 2, 4096, 1024], P('section', None, 'dp')
- section_grads: bfloat16 [4, 2, 4096, 1024], P('section', None, 'dp')
- param_grads: float32 [4, 8455168], P('section', 'dp')
- gain_grads: float32 [4, 1024], P('section')
The draws below stay inside these ranges and needn't reach their ends.
Inputs may be any that keep to these rules, and one draw needn't show every extreme that they name: `seq_lengths`: each row's lengths sum to 512; its first sequence has 256 tokens or more. `flat_params`: entries after a sub-layer's own matrices are zero.
All inputs are finite; a program needn't handle non-finite values.
Results may differ from the reference program's by a relative error of at most 0.023.
Values may be sent and summed in bfloat16 or wider, within the bound.
No kernel may reach another device: no remote copies, remote signals or barrier semaphores. Data moves between devices by JAX's collectives and lax.ppermute only.
A program may use at most 832 MiB of HBM per device.

```python
from functools import partial
import jax
import jax.numpy as jnp
from jax import lax

D = 1024
FF = 2752
HEADS = 16
FEAT = 16
WINDOW = 64
MICRO = 2
DOCS = 2
MB_TOK = 512
MIN_SEQ = 256
BLOCK = 512
BATCH_ROWS = 8
TOKENS = 4096
PARAMS = 8455168


def segment_plan(section_kind):
    fan_model = D ** (-0.5)
    if section_kind == 0:
        return [(D, 0.2, 1.0), (D * HEADS * FEAT, fan_model, 0.0), (D * HEADS * FEAT, fan_model, 0.0), (D * D, fan_model, 0.0), (D * D, 10.0 * fan_model, 0.0)]
    if section_kind == 2:
        return [(D, 0.2, 1.0), (D * D, fan_model, 0.0), (D * D, fan_model, 0.0), (D * D, fan_model, 0.0), (D * D, 4.0 * fan_model, 0.0)]
    return [(D, 0.2, 1.0), (D * FF, fan_model, 0.0), (D * FF, fan_model, 0.0), (FF * D, 2.0 * FF ** (-0.5), 0.0)]


def section_values(noise_draw, section_kind):
    positions = jnp.arange(PARAMS)
    spread = jnp.zeros((PARAMS,), jnp.float32)
    centre = jnp.zeros((PARAMS,), jnp.float32)
    offset = 0
    for length, deviation, middle in segment_plan(section_kind):
        inside = (positions >= offset) & (positions < offset + length)
        spread = jnp.where(inside, deviation, spread)
        centre = jnp.where(inside, middle, centre)
        offset += length
    return centre + spread * noise_draw


def draw_flat_params(key, part):
    key = jax.random.fold_in(key, 1)
    noise_draw = jax.random.truncated_normal(key, -4.0, 4.0, (4, PARAMS), jnp.float32)
    return jnp.stack([section_values(noise_draw[section_kind], section_kind) for section_kind in range(4)])


def draw_seq_lengths(key, part):
    key = jax.random.fold_in(key, 2)
    first_key, pick_key = jax.random.split(key)
    first_len = jax.random.randint(first_key, (MICRO, BATCH_ROWS), MIN_SEQ, MB_TOK)
    picked = jax.random.randint(pick_key, (MICRO, 1), 0, BATCH_ROWS)
    row_pos = jnp.arange(BATCH_ROWS, dtype=jnp.int32)[None, :]
    first_len = jnp.where(row_pos == picked, MB_TOK - 1, first_len)
    first_len = jnp.where(row_pos == (picked + 1) % BATCH_ROWS, MIN_SEQ, first_len)
    return jnp.stack([first_len, MB_TOK - first_len], axis=-1).astype(jnp.int32)


def shard_levels(own_key, extent, cuts, least, largest):
    loudness, own = 1.0, jax.random.fold_in(own_key, 6)
    for axis_at, shards_of in cuts:
        draws = jnp.exp(jax.random.uniform(jax.random.fold_in(own, axis_at), (shards_of,), jnp.float32, least / len(cuts), largest / len(cuts)))
        loudness = loudness * jnp.repeat(draws, extent[axis_at] // shards_of).reshape([-1 if axis == axis_at else 1 for axis in range(len(extent))])
    return loudness


def normal_values(key, dims, width, bound, cuts=(), kind=jnp.bfloat16):
    factor_of = shard_levels(key, dims, cuts, -0.22, 0.18) if cuts else 1.0
    values = jax.random.normal(key, dims, jnp.float32) * width * factor_of
    return jnp.minimum(jnp.maximum(values, -bound), bound).astype(kind)


def setup_inputs(seed: int = 0) -> dict:
    arg_keys = jax.random.split(jax.random.key(seed), 5)
    inputs = normal_values(arg_keys[0], (MICRO, TOKENS, D), 1.0, 6.0, ((1, 8),))
    cotangent = normal_values(arg_keys[1], (MICRO, TOKENS, D), 1.0, 6.0, ((1, 8),))
    seq_lengths = draw_seq_lengths(jax.random.fold_in(arg_keys[4], 71), 0)
    flat_params = draw_flat_params(jax.random.fold_in(arg_keys[4], 71), 0)
    return {"inputs": inputs, "cotangent": cotangent, "seq_lengths": seq_lengths, "flat_params": flat_params}


EPS = 1e-05
NEG_LARGE = -1e+30

@jax.custom_vjp
def low(v):
    return lax.optimization_barrier(v.astype(jnp.bfloat16)).astype(jnp.float32)

@jax.custom_vjp
def low_back(v):
    return v

def low_keep(v):
    return (low(v), None)

def low_pass(kept, grad):
    return (grad,)

def back_keep(v):
    return (v, None)

def back_low(kept, grad):
    return (low(grad),)
low.defvjp(low_keep, low_pass)
low_back.defvjp(back_keep, back_low)

def layout(section_kind):
    if section_kind == 0:
        return [(1, D), (D, HEADS * FEAT), (D, HEADS * FEAT), (D, D), (D, D)]
    if section_kind == 2:
        return [(1, D), (D, D), (D, D), (D, D), (D, D)]
    return [(1, D), (D, FF), (D, FF), (FF, D)]

def unpack(flat_vec, section_kind):
    pieces = []
    offset = 0
    for row_count, col_count in layout(section_kind):
        pieces.append(flat_vec[offset:offset + row_count * col_count].reshape(row_count, col_count))
        offset += row_count * col_count
    return pieces

def matmul_high(first_op, second_op):
    return jnp.dot(first_op, second_op, precision=lax.Precision.HIGHEST, preferred_element_type=jnp.float32)

def segment_ids(lengths):
    doc_ends = jnp.cumsum(lengths, axis=-1)
    positions = jnp.arange(MB_TOK, dtype=jnp.int32)
    return lax.optimization_barrier(jnp.sum((positions[None, :, None] >= doc_ends[:, None, :]).astype(jnp.int32), axis=-1))

def row_mix(section_kind, operands):
    query_rows, key_row_block, values, seg_row = operands
    score_scaling_factor = 0.25 if section_kind == 0 else 0.125
    outputs = []
    for start_row_index in range(0, MB_TOK, BLOCK):
        final_row_index = start_row_index + BLOCK
        score_matrix = low_back(jnp.einsum('ezl,jzl->zej', query_rows[start_row_index:final_row_index], key_row_block, precision=lax.Precision.HIGHEST) * score_scaling_factor)
        query_pos = start_row_index + jnp.arange(BLOCK, dtype=jnp.int32)
        key_pos = jnp.arange(MB_TOK, dtype=jnp.int32)
        allowed = (key_pos[None, :] <= query_pos[:, None]) & (seg_row[None, :] == seg_row[start_row_index:final_row_index][:, None])
        if section_kind == 0:
            weights = jnp.where(allowed[None], 1.0 + score_matrix + 0.5 * score_matrix * score_matrix, 0.0)
            soft_weights = low(weights / lax.optimization_barrier(jnp.sum(weights, axis=-1, keepdims=True)))
        else:
            allowed = allowed & (query_pos[:, None] - key_pos[None, :] < WINDOW)
            soft_weights = low(jax.nn.softmax(jnp.where(allowed[None], score_matrix, NEG_LARGE), axis=-1))
        outputs.append(jnp.einsum('hqk,khv->qhv', soft_weights, values, precision=lax.Precision.HIGHEST))
    return jnp.concatenate(outputs, axis=0)

def section_branch(section_kind, flat_vec, entry_val, segments):
    pieces = unpack(flat_vec, section_kind)
    rows_flat = entry_val.reshape(-1, D)
    normed = rows_flat * lax.rsqrt(lax.optimization_barrier(jnp.mean(rows_flat * rows_flat, axis=-1, keepdims=True)) + EPS) * pieces[0]
    hidden = low(normed)
    if section_kind == 1 or section_kind == 3:
        gate_proj = low_back(matmul_high(hidden, pieces[1]))
        up_proj = low_back(matmul_high(hidden, pieces[2]))
        activation = low(jax.nn.silu(gate_proj) * up_proj)
        return matmul_high(activation, pieces[3]).reshape(entry_val.shape)
    row_total = entry_val.shape[0]
    query_rows = low_back(low(matmul_high(hidden, pieces[1]))).reshape(row_total, MB_TOK, HEADS, -1)
    key_row_block = low_back(low(matmul_high(hidden, pieces[2]))).reshape(row_total, MB_TOK, HEADS, -1)
    values = low_back(low(matmul_high(hidden, pieces[3]))).reshape(row_total, MB_TOK, HEADS, -1)
    mixed_out = lax.map(jax.checkpoint(partial(row_mix, section_kind)), (query_rows, key_row_block, values, segments))
    mixed_out = low_back(low(mixed_out.reshape(-1, D)))
    return matmul_high(mixed_out, pieces[4]).reshape(entry_val.shape)

def reference(inputs, cotangent, seq_lengths, flat_params):
    row_total = MICRO * BATCH_ROWS
    start_rows = inputs.astype(jnp.float32).reshape(row_total, MB_TOK, D)
    grad_top = cotangent.astype(jnp.float32).reshape(row_total, MB_TOK, D)
    segments = segment_ids(seq_lengths.reshape(row_total, DOCS))

    def forward(weights, probes):
        rounded = low(weights)
        residual = start_rows
        outputs = []
        for section_kind in range(4):
            entry_val = low_back(residual + probes[section_kind])
            residual = low(entry_val + section_branch(section_kind, rounded[section_kind], entry_val, segments))
            outputs.append(residual)
        return (residual, jnp.stack(outputs))
    probes = jnp.zeros((4, row_total, MB_TOK, D), jnp.float32)
    final_rows, pullback, outputs = jax.vjp(forward, flat_params.astype(jnp.float32), probes, has_aux=True)
    grad_weights, grad_probes = pullback(grad_top)
    shape_out = (4, MICRO, TOKENS, D)
    return (outputs.reshape(shape_out).astype(jnp.bfloat16), grad_probes.reshape(shape_out).astype(jnp.bfloat16), grad_weights, grad_weights[:, 0:D])
```

```python
from functools import partial

import jax
import jax.numpy as jnp
import numpy as np
from jax import lax
from jax.experimental import pallas as pl
from jax.experimental.pallas import tpu as pltpu
from jax.sharding import PartitionSpec as P

D = 1024
FF = 2752
HEADS = 16
FEAT = 16
WINDOW = 64


EPS = 1e-05
NEG_LARGE = -1e30


def shortened(x):

    def short(part):
        return part.astype(jnp.bfloat16) if part.dtype == jnp.float32 else part

    return jax.tree.map(short, x)


def passed_along(value, axis, steps):
    count = lax.axis_size(axis)
    initial, last = (max(0, -steps), min(count, count - steps))
    return lax.ppermute(value, axis, [(source, source + steps) for source in range(initial, last)])


def layout(section_kind):
    if section_kind == 0:
        return [(1, D), (D, HEADS * FEAT), (D, HEADS * FEAT), (D, D), (D, D)]
    if section_kind == 2:
        return [(1, D), (D, D), (D, D), (D, D), (D, D)]
    return [(1, D), (D, FF), (D, FF), (FF, D)]


def unpack(flat_vec, section_kind):
    pieces = []
    offset = 0
    for row_count, col_count in layout(section_kind):
        pieces.append(
            flat_vec[offset : offset + row_count * col_count].reshape(row_count, col_count)
        )
        offset += row_count * col_count
    return pieces


def flatten_grads(grad_pieces, total_size):
    joined = jnp.concatenate([grad_piece.reshape(-1) for grad_piece in grad_pieces])
    return jnp.pad(joined, (0, total_size - joined.shape[0]))


def dot_plain(first_op, second_op):
    return jnp.dot(first_op, second_op, preferred_element_type=jnp.float32)


def dot_left(first_op, second_op):
    return lax.dot_general(
        first_op, second_op, (((0,), (0,)), ((), ())), preferred_element_type=jnp.float32
    )


def dot_right(first_op, second_op):
    return lax.dot_general(
        first_op, second_op, (((1,), (1,)), ((), ())), preferred_element_type=jnp.float32
    )


def segment_ids(lengths_row, total_rows):
    doc_ends = jnp.cumsum(lengths_row)
    positions = jnp.arange(total_rows, dtype=jnp.int32)
    return jnp.sum((positions[:, None] >= doc_ends[None, :]).astype(jnp.int32), axis=1)


def norm_forward(entry_val, gain_f32):
    inv_root = lax.rsqrt(jnp.mean(entry_val * entry_val, axis=-1, keepdims=True) + EPS)
    normed = entry_val * inv_root
    return (normed * gain_f32, normed, inv_root)


def norm_backward(grad_hidden, gain_f32, normed, inv_root):
    grad_normed = grad_hidden * gain_f32
    grad_gain = jnp.sum(grad_hidden * normed, axis=0, keepdims=True)
    grad_entry = inv_root * (
        grad_normed - normed * jnp.mean(grad_normed * normed, axis=-1, keepdims=True)
    )
    return (grad_entry, grad_gain)


def block_weights(section_kind, query_rows, key_row_block, seg_ids, start_row_index, block_size):
    final_row_index = start_row_index + block_size
    first_key = 0 if section_kind == 0 else max(0, start_row_index - WINDOW)
    score_scaling_factor = 0.25 if section_kind == 0 else 0.125
    score_matrix = (
        jnp.einsum(
            "ezl,jzl->zej",
            query_rows[start_row_index:final_row_index],
            key_row_block[first_key:final_row_index],
            preferred_element_type=jnp.float32,
        )
        * score_scaling_factor
    )
    query_pos = start_row_index + jnp.arange(block_size, dtype=jnp.int32)
    key_pos = first_key + jnp.arange(final_row_index - first_key, dtype=jnp.int32)
    allowed = (key_pos[None, :] <= query_pos[:, None]) & (
        seg_ids[first_key:final_row_index][None, :]
        == seg_ids[start_row_index:final_row_index][:, None]
    )
    if section_kind == 0:
        weights = jnp.where(
            allowed[None], 1.0 + score_matrix + 0.5 * score_matrix * score_matrix, 0.0
        )
        totals = jnp.sum(weights, axis=-1, keepdims=True)
        return (score_matrix, allowed, weights / totals, totals, first_key)
    allowed = allowed & (query_pos[:, None] - key_pos[None, :] < WINDOW)
    masked = jnp.where(allowed[None], score_matrix, NEG_LARGE)
    exponent = jnp.where(
        allowed[None], jnp.exp(masked - jnp.max(masked, axis=-1, keepdims=True)), 0.0
    )
    totals = jnp.sum(exponent, axis=-1, keepdims=True)
    return (score_matrix, allowed, exponent / totals, totals, first_key)


def mix_forward(section_kind, query_rows, key_row_block, values, seg_ids):
    row_total = query_rows.shape[0]
    block_size = min(512, row_total)
    outputs = []
    for start_row_index in range(0, row_total, block_size):
        score_matrix, allowed, soft_weights, totals, first_key = block_weights(
            section_kind, query_rows, key_row_block, seg_ids, start_row_index, block_size
        )
        outputs.append(
            jnp.einsum(
                "hqk,khv->qhv",
                soft_weights.astype(jnp.bfloat16),
                values[first_key : start_row_index + block_size],
                preferred_element_type=jnp.float32,
            )
        )
    return jnp.concatenate(outputs, axis=0).astype(jnp.bfloat16)


def mix_backward(section_kind, query_rows, key_row_block, values, seg_ids, grad_mixed):
    row_total = query_rows.shape[0]
    block_size = min(512, row_total)
    score_scaling_factor = 0.25 if section_kind == 0 else 0.125
    grad_query_parts = []
    mixed_parts = []
    grad_keys = jnp.zeros(key_row_block.shape, jnp.float32)
    grad_values = jnp.zeros(values.shape, jnp.float32)
    for start_row_index in range(0, row_total, block_size):
        final_row_index = start_row_index + block_size
        score_matrix, allowed, soft_weights, totals, first_key = block_weights(
            section_kind, query_rows, key_row_block, seg_ids, start_row_index, block_size
        )
        rounded_weights = soft_weights.astype(jnp.bfloat16)
        value_block = values[first_key:final_row_index]
        grad_block = grad_mixed[start_row_index:final_row_index]
        mixed_parts.append(
            jnp.einsum(
                "hqk,khv->qhv", rounded_weights, value_block, preferred_element_type=jnp.float32
            )
        )
        grad_values = grad_values.at[first_key:final_row_index].add(
            jnp.einsum(
                "hqk,qhv->khv", rounded_weights, grad_block, preferred_element_type=jnp.float32
            )
        )
        grad_weights = jnp.einsum(
            "qhv,khv->hqk", grad_block, value_block, preferred_element_type=jnp.float32
        )
        centred = grad_weights - jnp.sum(grad_weights * soft_weights, axis=-1, keepdims=True)
        if section_kind == 0:
            grad_scores = jnp.where(allowed[None], centred * (1.0 + score_matrix) / totals, 0.0)
        else:
            grad_scores = jnp.where(allowed[None], soft_weights * centred, 0.0)
        grad_scores = grad_scores.astype(jnp.bfloat16)
        grad_query_parts.append(
            jnp.einsum(
                "ncw,wne->cne",
                grad_scores,
                key_row_block[first_key:final_row_index],
                preferred_element_type=jnp.float32,
            )
            * score_scaling_factor
        )
        grad_keys = grad_keys.at[first_key:final_row_index].add(
            jnp.einsum(
                "zas,aze->sze",
                grad_scores,
                query_rows[start_row_index:final_row_index],
                preferred_element_type=jnp.float32,
            )
            * score_scaling_factor
        )
    mixed_out = jnp.concatenate(mixed_parts, axis=0).astype(jnp.bfloat16)
    grad_query = jnp.concatenate(grad_query_parts, axis=0).astype(jnp.bfloat16)
    return (mixed_out, grad_query, grad_keys.astype(jnp.bfloat16), grad_values.astype(jnp.bfloat16))


def attention_setup(flat_vec, residual, section_kind):
    norm_gain, w_query, w_key, w_value, w_out = unpack(flat_vec, section_kind)
    entry_val = residual.astype(jnp.float32)
    gain_f32 = norm_gain.astype(jnp.float32)
    normed_out, normed, inv_root = norm_forward(entry_val, gain_f32)
    hidden = normed_out.astype(jnp.bfloat16)
    row_total = residual.shape[0]
    query_rows = dot_plain(hidden, w_query).astype(jnp.bfloat16).reshape(row_total, HEADS, -1)
    key_row_block = dot_plain(hidden, w_key).astype(jnp.bfloat16).reshape(row_total, HEADS, -1)
    values = dot_plain(hidden, w_value).astype(jnp.bfloat16).reshape(row_total, HEADS, -1)
    return (
        w_query,
        w_key,
        w_value,
        w_out,
        entry_val,
        gain_f32,
        normed,
        inv_root,
        hidden,
        query_rows,
        key_row_block,
        values,
    )


def attention_forward(flat_vec, residual, seg_ids, section_kind):
    (
        w_query,
        w_key,
        w_value,
        w_out,
        entry_val,
        gain_f32,
        normed,
        inv_root,
        hidden,
        query_rows,
        key_row_block,
        values,
    ) = attention_setup(flat_vec, residual, section_kind)
    mixed_out = mix_forward(section_kind, query_rows, key_row_block, values, seg_ids)
    branch_out = dot_plain(mixed_out.reshape(residual.shape[0], -1), w_out)
    return (entry_val + branch_out).astype(jnp.bfloat16)


def attention_backward(flat_vec, residual, seg_ids, grad_out, section_kind):
    (
        w_query,
        w_key,
        w_value,
        w_out,
        entry_val,
        gain_f32,
        normed,
        inv_root,
        hidden,
        query_rows,
        key_row_block,
        values,
    ) = attention_setup(flat_vec, residual, section_kind)
    row_total = residual.shape[0]
    grad_mixed = dot_right(grad_out, w_out).astype(jnp.bfloat16).reshape(row_total, HEADS, -1)
    mixed_out, grad_query, grad_keys, grad_values = mix_backward(
        section_kind, query_rows, key_row_block, values, seg_ids, grad_mixed
    )
    grad_w_out = dot_left(mixed_out.reshape(row_total, -1), grad_out)
    grad_query = grad_query.reshape(row_total, -1)
    grad_keys = grad_keys.reshape(row_total, -1)
    grad_values = grad_values.reshape(row_total, -1)
    grad_hidden = (
        dot_right(grad_query, w_query)
        + dot_right(grad_keys, w_key)
        + dot_right(grad_values, w_value)
    )
    grad_entry, grad_gain = norm_backward(grad_hidden, gain_f32, normed, inv_root)
    grad_in = (grad_out.astype(jnp.float32) + grad_entry).astype(jnp.bfloat16)
    grad_flat = flatten_grads(
        [
            grad_gain,
            dot_left(hidden, grad_query),
            dot_left(hidden, grad_keys),
            dot_left(hidden, grad_values),
            grad_w_out,
        ],
        flat_vec.shape[0],
    )
    return (grad_in, grad_flat)


def mlp_setup(flat_vec, residual):
    norm_gain, w_gate, w_up, w_down = unpack(flat_vec, 1)
    entry_val = residual.astype(jnp.float32)
    gain_f32 = norm_gain.astype(jnp.float32)
    normed_out, normed, inv_root = norm_forward(entry_val, gain_f32)
    hidden = normed_out.astype(jnp.bfloat16)
    gate_pre = dot_plain(hidden, w_gate)
    up_pre = dot_plain(hidden, w_up)
    return (w_gate, w_up, w_down, entry_val, gain_f32, normed, inv_root, hidden, gate_pre, up_pre)


def mlp_forward(flat_vec, residual, seg_ids):
    w_gate, w_up, w_down, entry_val, gain_f32, normed, inv_root, hidden, gate_pre, up_pre = (
        mlp_setup(flat_vec, residual)
    )
    activation = (jax.nn.silu(gate_pre) * up_pre).astype(jnp.bfloat16)
    return (entry_val + dot_plain(activation, w_down)).astype(jnp.bfloat16)


def mlp_backward(flat_vec, residual, seg_ids, grad_out):
    w_gate, w_up, w_down, entry_val, gain_f32, normed, inv_root, hidden, gate_pre, up_pre = (
        mlp_setup(flat_vec, residual)
    )
    sigmoid_gate = jax.nn.sigmoid(gate_pre)
    silu_gate = gate_pre * sigmoid_gate
    activation = (silu_gate * up_pre).astype(jnp.bfloat16)
    grad_w_down = dot_left(activation, grad_out)
    grad_activation = dot_right(grad_out, w_down)
    grad_gate = (
        grad_activation * up_pre * sigmoid_gate * (1.0 + gate_pre * (1.0 - sigmoid_gate))
    ).astype(jnp.bfloat16)
    grad_up = (grad_activation * silu_gate).astype(jnp.bfloat16)
    grad_hidden = dot_right(grad_gate, w_gate) + dot_right(grad_up, w_up)
    grad_entry, grad_gain = norm_backward(grad_hidden, gain_f32, normed, inv_root)
    grad_in = (grad_out.astype(jnp.float32) + grad_entry).astype(jnp.bfloat16)
    grad_flat = flatten_grads(
        [grad_gain, dot_left(hidden, grad_gate), dot_left(hidden, grad_up), grad_w_down],
        flat_vec.shape[0],
    )
    return (grad_in, grad_flat)


def spare_forward(flat_vec, residual, seg_ids):
    return jnp.zeros_like(residual)


def spare_backward(flat_vec, residual, seg_ids, grad_out):
    return (jnp.zeros_like(residual), jnp.zeros(flat_vec.shape, jnp.float32))


def store_slot(buffer, new_value, slot_index, active):
    current = lax.dynamic_index_in_dim(buffer, slot_index, 0, keepdims=False)
    return lax.dynamic_update_slice_in_dim(
        buffer, jnp.where(active, new_value, current)[None], slot_index, 0
    )


def per_device(inputs, cotangent, seq_lengths, flat_params):
    section_now = lax.axis_index("section")
    section_count = lax.axis_size("section")
    micro_count = inputs.shape[0]
    row_total = inputs.shape[1]
    shard_low = flat_params.astype(jnp.bfloat16)
    gathered = lax.all_gather(shard_low, "dp", axis=1, tiled=True)[0]
    forward_fns = [
        partial(attention_forward, section_kind=0),
        mlp_forward,
        partial(attention_forward, section_kind=2),
        mlp_forward,
        spare_forward,
    ]
    backward_fns = [
        partial(attention_backward, section_kind=0),
        mlp_backward,
        partial(attention_backward, section_kind=2),
        mlp_backward,
        spare_backward,
    ]
    saved_inputs = jnp.zeros_like(inputs)
    produced = jnp.zeros_like(inputs)
    previous = jnp.zeros(inputs.shape[1:], jnp.bfloat16)
    for tick_step in range(micro_count + section_count - 1):
        micro_index = tick_step - section_now
        active = (micro_index >= 0) & (micro_index < micro_count)
        chosen = jnp.clip(micro_index, 0, micro_count - 1)
        if tick_step > 0:
            arrived = jax.tree.map(
                lambda part, own: part.astype(own.dtype),
                passed_along(shortened(previous), "section", 1),
                previous,
            )
        else:
            arrived = previous
        residual = jnp.where(
            section_now == 0, lax.dynamic_index_in_dim(inputs, chosen, 0, keepdims=False), arrived
        )
        lengths_row = lax.dynamic_index_in_dim(seq_lengths, chosen, 0, keepdims=False)[0]
        seg_ids = segment_ids(lengths_row, row_total)
        branch_index = jnp.where(active, section_now, 4)
        result = lax.switch(branch_index, forward_fns, gathered, residual, seg_ids)
        saved_inputs = store_slot(saved_inputs, residual, chosen, active)
        produced = store_slot(produced, result, chosen, active)
        previous = result
    back_weights = lax.all_gather(shard_low, "dp", axis=1, tiled=True)[0]
    grads_in = jnp.zeros_like(inputs)
    grad_total = jnp.zeros(gathered.shape, jnp.float32)
    gain_total = jnp.zeros((D,), jnp.float32)
    previous_grad = jnp.zeros(inputs.shape[1:], jnp.bfloat16)
    for tick_step in range(micro_count + section_count - 1):
        micro_index = micro_count - 1 - tick_step + (section_count - 1 - section_now)
        active = (micro_index >= 0) & (micro_index < micro_count)
        chosen = jnp.clip(micro_index, 0, micro_count - 1)
        if tick_step > 0:
            arrived = jax.tree.map(
                lambda part, own: part.astype(own.dtype),
                passed_along(shortened(previous_grad), "section", -1),
                previous_grad,
            )
        else:
            arrived = previous_grad
        grad_out = jnp.where(
            section_now == section_count - 1,
            lax.dynamic_index_in_dim(cotangent, chosen, 0, keepdims=False),
            arrived,
        )
        residual = lax.dynamic_index_in_dim(saved_inputs, chosen, 0, keepdims=False)
        lengths_row = lax.dynamic_index_in_dim(seq_lengths, chosen, 0, keepdims=False)[0]
        seg_ids = segment_ids(lengths_row, row_total)
        branch_index = jnp.where(active, section_now, 4)
        grad_in, grad_flat = lax.switch(
            branch_index, backward_fns, back_weights, residual, seg_ids, grad_out
        )
        grads_in = store_slot(grads_in, grad_in, chosen, active)
        gain_total = gain_total + grad_flat[0:D]
        grad_total = grad_total + grad_flat
        previous_grad = grad_in
    shard_total = lax.psum_scatter(grad_total[None], "dp", scatter_dimension=1, tiled=True)
    gain_grads = lax.psum(gain_total, "dp")[None]
    return (produced[None], grads_in[None], shard_total, gain_grads)


AXES = ("y", "x", "z", "c")
GROUP = ("y", "z", "c")
DEPTH = 4
WIDE = 1408
TILE = 128
STRETCHES = ((0, 172, 176), (688, 258, 264), (1720, 258, 264))
bf16 = jnp.bfloat16
f32 = jnp.float32


def unit_columns(half):
    order = []
    for first, count, padded in STRETCHES:
        for part in (2 * half, 2 * half + 1):
            start = first + count * part
            order += list(range(start, start + count)) + [-1] * (padded - count)
    return order


COLUMNS = np.array(unit_columns(0) + unit_columns(1), np.int32)


def route(value, rule):
    pairs = []
    for y in range(2):
        for x in range(2):
            for z in range(DEPTH):
                for c in range(2):
                    target = rule(y, x, z, c)
                    if target is not None:
                        ty, tx, tz, tc = target
                        pairs.append((((2 * y + x) * DEPTH + z) * 2 + c, ((2 * ty + tx) * DEPTH + tz) * 2 + tc))
    return lax.ppermute(value, AXES, pairs)


def swap_x(value):
    return route(value, lambda y, x, z, c: (y, 1 - x, z, c))


def swap_y(value):
    return route(value, lambda y, x, z, c: (1 - y, x, z, c))


def swap_xy(value):
    return route(value, lambda y, x, z, c: (1 - y, 1 - x, z, c))


def swap_c(value):
    return route(value, lambda y, x, z, c: (y, x, z, 1 - c))


def along_z(value, moves):
    return route(value, lambda y, x, z, c: (y, x, moves[z], c) if z in moves else None)


def spot(y, z, c):
    return (y * DEPTH + z) * 2 + c


def by_index(index, choices):
    result = choices[-1]
    for i in range(len(choices) - 2, -1, -1):
        result = jnp.where(index == i, choices[i], result)
    return result


def tied(*values):
    spec = pl.BlockSpec(memory_space=pl.ANY)
    return pl.pallas_call(
        lambda *refs: None,
        in_specs=[spec] * len(values),
        out_specs=[spec] * len(values),
        out_shape=[jax.ShapeDtypeStruct(value.shape, value.dtype) for value in values],
        input_output_aliases={i: i for i in range(len(values))},
    )(*values)


def lane_mask(width, lanes, index):
    return (lax.broadcasted_iota(jnp.int32, (1, lanes), 1) // width) == index


def dot_nt(a, b):
    return lax.dot_general(a, b, (((1,), (1,)), ((), ())), preferred_element_type=f32)


def dot_tn(a, b):
    return lax.dot_general(a, b, (((0,), (0,)), ((), ())), preferred_element_type=f32)


def pair_mask(row_seg, col_seg, row_start, rows, key_start, keys, window):
    query_pos = row_start + lax.broadcasted_iota(jnp.int32, (rows, keys), 0)
    key_pos = key_start + lax.broadcasted_iota(jnp.int32, (rows, keys), 1)
    allowed = (key_pos <= query_pos) & (
        col_seg[row_start : row_start + rows, :] == row_seg[:, key_start : key_start + keys]
    )
    if window:
        allowed = allowed & (query_pos - key_pos < window)
    return allowed


def tiles(taylor, row_total):
    step = 256 if taylor else 128
    reach = row_total if taylor else 128
    return [(start, step, max(0, start - reach)) for start in range(0, row_total, step)]


def probabilities(taylor, score, allowed):
    if taylor:
        poly = jnp.where(allowed, 1.0 + score + 0.5 * score * score, 0.0)
        inv_total = 1.0 / jnp.sum(poly, axis=-1, keepdims=True)
        return poly * inv_total, inv_total
    masked = jnp.where(allowed, score, NEG_LARGE)
    expo = jnp.where(allowed, jnp.exp(masked - jnp.max(masked, axis=-1, keepdims=True)), 0.0)
    inv_total = 1.0 / jnp.sum(expo, axis=-1, keepdims=True)
    return expo * inv_total, inv_total


def mix_kernel(taylor, row_seg_ref, col_seg_ref, q_ref, k_ref, v_ref, out_ref):
    row_seg, col_seg = row_seg_ref[...], col_seg_ref[...]
    row_total = q_ref.shape[0]
    for start, rows, first in tiles(taylor, row_total):
        keys = start + rows - first
        allowed = pair_mask(row_seg, col_seg, start, rows, first, keys, 0 if taylor else WINDOW)
        for pair in range(v_ref.shape[1] // 128):
            lanes = slice(128 * pair, 128 * pair + 128)
            narrow = slice(0, 128) if taylor else lanes
            outs = []
            for j in range(2):
                qk_mask = lane_mask(16, 128, 2 * pair + j) if taylor else lane_mask(64, 128, j)
                q = jnp.where(qk_mask, q_ref[start : start + rows, narrow], 0).astype(bf16)
                score = dot_nt(q, k_ref[first : first + keys, narrow]) * (0.25 if taylor else 0.125)
                probs, _ = probabilities(taylor, score, allowed)
                outs.append(
                    jnp.dot(probs.astype(bf16), v_ref[first : first + keys, lanes], preferred_element_type=f32)
                )
            out_ref[start : start + rows, lanes] = jnp.where(lane_mask(64, 128, 0), outs[0], outs[1]).astype(bf16)


def mix_grad_kernel(
    taylor, row_seg_ref, col_seg_ref, q_ref, k_ref, v_ref, gm_ref, gq_ref, gk_ref, gv_ref, aq, ak, av
):
    row_seg, col_seg = row_seg_ref[...], col_seg_ref[...]
    row_total = q_ref.shape[0]
    scale = 0.25 if taylor else 0.125
    aq[...] = jnp.zeros_like(aq)
    ak[...] = jnp.zeros_like(ak)
    av[...] = jnp.zeros_like(av)
    for start, rows, first in tiles(taylor, row_total):
        stop = start + rows
        keys = stop - first
        allowed = pair_mask(row_seg, col_seg, start, rows, first, keys, 0 if taylor else WINDOW)
        for pair in range(v_ref.shape[1] // 128):
            lanes = slice(128 * pair, 128 * pair + 128)
            narrow = slice(0, 128) if taylor else lanes
            for j in range(2):
                qk_mask = lane_mask(16, 128, 2 * pair + j) if taylor else lane_mask(64, 128, j)
                q = jnp.where(qk_mask, q_ref[start:stop, narrow], 0).astype(bf16)
                k = jnp.where(qk_mask, k_ref[first:stop, narrow], 0).astype(bf16)
                gm = jnp.where(lane_mask(64, 128, j), gm_ref[start:stop, lanes], 0).astype(bf16)
                score = dot_nt(q, k) * scale
                probs, inv_total = probabilities(taylor, score, allowed)
                grad_probs = dot_nt(gm, v_ref[first:stop, lanes])
                centred = grad_probs - jnp.sum(grad_probs * probs, axis=-1, keepdims=True)
                if taylor:
                    grad_score = jnp.where(allowed, centred * (1.0 + score) * inv_total, 0.0)
                else:
                    grad_score = probs * centred
                grad_score = grad_score.astype(bf16)
                aq[start:stop, narrow] += jnp.dot(grad_score, k, preferred_element_type=f32) * scale
                ak[first:stop, narrow] += dot_tn(grad_score, q) * scale
                av[first:stop, lanes] += dot_tn(probs.astype(bf16), gm)
    gq_ref[...] = aq[...].astype(bf16)
    gk_ref[...] = ak[...].astype(bf16)
    gv_ref[...] = av[...].astype(bf16)


def mix(taylor, seg_ids, q, k, v):
    return pl.pallas_call(
        partial(mix_kernel, taylor),
        in_specs=[pl.BlockSpec(memory_space=pltpu.VMEM)] * 5,
        out_shape=jax.ShapeDtypeStruct(v.shape, bf16),
        compiler_params=pltpu.CompilerParams(vmem_limit_bytes=32 * 2**20),
        cost_estimate=pl.CostEstimate(flops=2**30, bytes_accessed=2**21, transcendentals=0),
    )(seg_ids[None, :], seg_ids[:, None], q, k, v)


def mix_grad(taylor, seg_ids, q, k, v, gm):
    return pl.pallas_call(
        partial(mix_grad_kernel, taylor),
        in_specs=[pl.BlockSpec(memory_space=pltpu.VMEM)] * 6,
        out_shape=[jax.ShapeDtypeStruct(a.shape, bf16) for a in (q, k, v)],
        scratch_shapes=[pltpu.VMEM(a.shape, f32) for a in (q, k, v)],
        compiler_params=pltpu.CompilerParams(vmem_limit_bytes=32 * 2**20),
        cost_estimate=pl.CostEstimate(flops=3 * 2**30, bytes_accessed=2**22, transcendentals=0),
    )(seg_ids[None, :], seg_ids[:, None], q, k, v, gm)


SHARD = 8257
LINED = 8256
LEFT = 192
UNIT = 1024
ROWS = 2176
GAIN = 16
PAIR = 43


def pieces(position, count, table):
    found = []
    for place in range(count):
        number = int(table[position + place])
        if number < 0:
            continue
        if found and found[-1][1] == place and found[-1][2] + place - found[-1][0] == number:
            found[-1][1] = place + 1
        else:
            found.append([place, place + 1, number])
    return found


def shifted(load, position, last):
    row, shift = position // TILE, position % TILE
    near = load(min(max(row, 0), last))
    if shift == 0:
        return near
    far = load(min(max(row + 1, 0), last))
    lane = lax.broadcasted_iota(jnp.int32, near.shape, 1)
    return pltpu.roll(jnp.where(lane >= shift, near, far), TILE - shift, 1)


def between_lanes(shape, low, high):
    lane = lax.broadcasted_iota(jnp.int32, shape, 1)
    return (lane >= low) & (lane < high)


def masked_rows(value, rows):
    row = lax.broadcasted_iota(jnp.int32, value.shape, 0)
    return jnp.where(row < rows, value, 0.0)


def unit_stretches(owner_y, d, half):
    if owner_y == 1:
        if d == 3:
            return [(512 * half, 0, 1), (512 * half, 4, 1)]
        return [(0, 4 * half, 1), (512, 4 * half, 1)]
    if d == 0:
        return [(0, half, 2), (512, 4 * half, 1)]
    if d == 1:
        return [(0, 4 * half, 1), None]
    return [(0, 0, 1), (0, 4, 1)] if half else [None, None]


UNIT_CASES = [
    (1, 0, lambda y, d: (y == 1) & (d < 3)),
    (1, 3, lambda y, d: (y == 1) & (d == 3)),
    (0, 0, lambda y, d: (y == 0) & (d == 0)),
    (0, 1, lambda y, d: (y == 0) & (d == 1)),
    (0, 2, lambda y, d: (y == 0) & (d == 2)),
]


def source_kernel(info_ref, flat_ref, left_ref, right_ref, out_ref, moved_ref, buf, column, sem):
    copy = pltpu.make_async_copy(flat_ref.reshape(SHARD, TILE), buf.at[pl.ds(LEFT, SHARD)], sem)
    copy.start()
    buf[:LEFT, :] = left_ref[...]
    copy.wait()
    buf[LEFT + SHARD : LEFT + SHARD + 8, :] = right_ref[...]
    start, x, y, d = info_ref[0], info_ref[1], info_ref[2], info_ref[3]
    gain = buf[LEFT : LEFT + GAIN, :].astype(bf16)

    for owner_y, unit_d, chosen in UNIT_CASES:

        @pl.when((x == 0) & chosen(y, d))
        def _(owner_y=owner_y, unit_d=unit_d):
            for half in range(2):
                for k in range(4):
                    part, deep = k % 2, k // 2
                    place, base = half * 2 + (part ^ owner_y), deep * (UNIT + GAIN)
                    for side, stretch in enumerate(unit_stretches(owner_y, unit_d, half)):
                        if stretch is not None:
                            row, strip, step = stretch
                            value = buf[pl.ds(start + 8 * row + strip + step * k, 512, stride=8), :]
                            out_ref[place, base + 512 * side : base + 512 * side + 512, :] = value.astype(bf16)
                    out_ref[place, base + UNIT : base + UNIT + GAIN, :] = gain
            if (owner_y, unit_d) == (0, 1):
                for k in range(4):
                    for side in range(2):
                        value = buf[pl.ds(start + 8 * 512 + 4 * side + k, 512, stride=8), :]
                        row = (k // 2) * (UNIT + GAIN) + 512 * side
                        moved_ref[k % 2, row : row + 512, :] = value.astype(bf16)

    @pl.when((x == 1) & (d <= 5))
    def _():
        for half in range(2):
            for j in range(WIDE // TILE):
                for parity in range(2):
                    load = lambda row: buf[pl.ds(start + row, 192, stride=PAIR), :]
                    value = jnp.zeros((192, TILE), f32)
                    for low, high, number in pieces(WIDE * half + TILE * j, TILE, COLUMNS):
                        got = shifted(load, parity * FF + number - low, PAIR)
                        value = jnp.where(between_lanes(value.shape, low, high), got, value)
                    column[pl.ds(parity, 192, stride=2), :] = value
                whole = column[...].astype(bf16)

                @pl.when(d <= 4)
                def _():
                    for r in range(3):
                        t = 11 * r + j
                        part, place = (0, t) if t < 17 else (1, t - 17)
                        out_ref[(1 - half) * 2 + (y ^ part), TILE * place : TILE * place + TILE, :] = whole[
                            TILE * r : TILE * r + TILE
                        ]

                @pl.when(d == 5)
                def _():
                    part, place = (0, j) if j < 6 else (1, j - 6)
                    out_ref[(1 - half) * 2 + (y ^ part), TILE * place : TILE * place + TILE, :] = whole[:TILE]

    @pl.when(x == 1)
    def _():
        for half in range(2):
            for part in range(2):
                q, place = 2 * half + part, (1 - half) * 2 + (y ^ part)
                out_ref[place, ROWS : ROWS + GAIN, :] = gain

                @pl.when(d == 5)
                def _():
                    for j in range(8):
                        value = buf[pl.ds(start + 8 * (344 + 172 * q) + j, 176, stride=8), :]
                        first = (6, 5)[part] * TILE + 176 * j
                        out_ref[place, first : first + 176, :] = masked_rows(value, 172).astype(bf16)

                @pl.when(d > 5)
                def _():
                    for j in range(8):
                        value = buf[pl.ds(start + 8 * 258 * q + j, 272, stride=8), :]
                        out_ref[place, 272 * j : 272 * j + 272, :] = masked_rows(value, 258).astype(bf16)


def line_kernel(info_ref, *refs):
    block_refs, moved_refs, out_ref, halves = refs[:4], refs[4:6], refs[8], refs[9]
    x, y, d = info_ref[0], info_ref[1], info_ref[2]

    @pl.when(x == 0)
    def _():
        out_ref[...] = jnp.zeros_like(out_ref)

    for owner_y, unit_d, chosen in UNIT_CASES:

        @pl.when((x == 0) & chosen(y, d))
        def _(owner_y=owner_y, unit_d=unit_d):
            for half in range(2):
                for k in range(4):
                    part, deep = k % 2, k // 2
                    ref, base = block_refs[half * 2 + (part ^ owner_y)], UNIT * deep
                    for side, stretch in enumerate(unit_stretches(owner_y, unit_d, half)):
                        if stretch is not None:
                            row, strip, step = stretch
                            value = ref[base + 512 * side : base + 512 * side + 512, :].astype(f32)
                            out_ref[pl.ds(8 * row + strip + step * k, 512, stride=8), :] = value
            if (owner_y, unit_d) == (0, 1):
                for k in range(4):
                    for side in range(2):
                        row = UNIT * (k // 2) + 512 * side
                        value = moved_refs[k % 2][row : row + 512, :].astype(f32)
                        out_ref[pl.ds(8 * 512 + 4 * side + k, 512, stride=8), :] = value

    inverse = np.full((2 * FF,), -1, np.int64)
    for place, number in enumerate(COLUMNS):
        if number >= 0:
            inverse[number] = place
            inverse[FF + number] = 2 * WIDE + place

    for own_y in range(2):

        @pl.when((x == 1) & (d <= 5) & (y == own_y))
        def _(own_y=own_y):
            for half in range(2):
                ref = [block_refs[(1 - half) * 2 + (part ^ own_y)] for part in range(2)]

                @pl.when(d <= 4)
                def _():
                    for t in range(33):
                        part, place = (0, t) if t < 17 else (1, t - 17)
                        r, j = t // 11, t % 11
                        halves[11 * half + j, TILE * r : TILE * r + TILE, :] = ref[part][
                            TILE * place : TILE * place + TILE, :
                        ].astype(f32)

                @pl.when(d == 5)
                def _():
                    for j in range(11):
                        part, place = (0, j) if j < 6 else (1, j - 6)
                        halves[11 * half + j, :TILE, :] = ref[part][
                            TILE * place : TILE * place + TILE, :
                        ].astype(f32)

    @pl.when((x == 1) & (d <= 5))
    def _():
        for b in range(PAIR):
            value = jnp.zeros((192, TILE), f32)
            for low, high, number in pieces(TILE * b, TILE, inverse):
                parity, rest = number // (2 * WIDE), number % (2 * WIDE)
                half, local = rest // WIDE, rest % WIDE
                load = lambda j: halves[11 * half + j, pl.ds(parity, 192, stride=2), :]
                got = shifted(load, local - low, WIDE // TILE - 1)
                value = jnp.where(between_lanes(value.shape, low, high), got, value)
            out_ref[pl.ds(b, 192, stride=PAIR), :] = value

    for own_y in range(2):

        @pl.when((x == 1) & (d >= 5) & (y == own_y))
        def _(own_y=own_y):
            for q in range(4):
                half, part = q // 2, q % 2
                ref = block_refs[(1 - half) * 2 + (part ^ own_y)]

                @pl.when(d == 5)
                def _():
                    for j in range(8):
                        first = (6, 5)[part] * TILE + 176 * j
                        value = ref[first : first + 176, :].astype(f32)
                        out_ref[pl.ds(8 * (344 + 172 * q) + j, 176, stride=8), :] = value

                @pl.when(d > 5)
                def _():
                    for j in range(8):
                        value = ref[272 * j : 272 * j + 272, :].astype(f32)
                        out_ref[pl.ds(8 * 258 * q + j, 264, stride=8), :] = value[:264]


def flat_kernel(start_ref, lined_ref, left_ref, right_ref, out_ref, buf, staged, sem):
    buf[:8, :] = left_ref[...]
    buf[8 : 8 + LINED, :] = lined_ref[:LINED, :]
    buf[8 + LINED :, :] = jnp.zeros((buf.shape[0] - 8 - LINED, 128), f32)

    @pl.when(start_ref[1] == 0)
    def _():
        buf[8 + 8192 : 8 + 8192 + 256, :] = right_ref[...]

    staged[...] = buf[pl.ds(start_ref[0], SHARD), :]
    copy = pltpu.make_async_copy(staged, out_ref.reshape(SHARD, 128), sem)
    copy.start()
    copy.wait()


def padded(m, rows):
    return jnp.pad(m, ((0, rows - m.shape[0]), (0, 0)))


def dp_right(value):
    return lax.ppermute(value, AXES, [(8 * s + i, 8 * s + i + 1) for s in range(4) for i in range(7)])


def dp_left(value):
    return lax.ppermute(value, AXES, [(8 * s + i + 1, 8 * s + i) for s in range(4) for i in range(7)])


def source_blocks(flat_params, y, x, z, c, d):
    tail = flat_params[:, -LEFT * 128 :].reshape(LEFT, 128)
    head = flat_params[:, :1024].reshape(8, 128)
    left, right = dp_right(tail), dp_left(head)
    start = jnp.maximum(200 - jnp.where(x == 0, 65 * d, d), 0)
    blocks, moved = pl.pallas_call(
        source_kernel,
        in_specs=[
            pl.BlockSpec(memory_space=pltpu.SMEM),
            pl.BlockSpec(memory_space=pl.ANY),
            pl.BlockSpec(memory_space=pltpu.VMEM),
            pl.BlockSpec(memory_space=pltpu.VMEM),
        ],
        out_shape=[
            jax.ShapeDtypeStruct((4, ROWS + GAIN, TILE), bf16),
            jax.ShapeDtypeStruct((2, ROWS + GAIN, TILE), bf16),
        ],
        scratch_shapes=[pltpu.VMEM((8576, TILE), f32), pltpu.VMEM((384, TILE), f32), pltpu.SemaphoreType.DMA],
        compiler_params=pltpu.CompilerParams(vmem_limit_bytes=40 * 2**20),
    )(jnp.stack([start, x, y, d]), flat_params, left, right)
    moved = route(moved, lambda yy, xx, zz, cc: (0, 0, 1, 0) if (yy, xx, zz, cc) == (0, 0, 0, 1) else None)
    from_x, from_xy = swap_x(blocks[2]), swap_xy(blocks[3])
    swapped = (y == 0) & (x == 0) & (d == 2)
    own, flipped = jnp.where(swapped, moved[0], blocks[0]), jnp.where(swapped, moved[1], blocks[1])
    from_y = swap_y(flipped)
    own_units, own_rows = jnp.where(x == 0, own, from_x), jnp.where(x == 0, from_x, own)
    other_units, other_rows = jnp.where(x == 0, from_y, from_xy), jnp.where(x == 0, from_xy, from_y)
    size = UNIT + GAIN

    pick = lambda owner, own, other: jnp.where(y == owner, own, other)
    units = [pick(owner, own_units, other_units) for owner in (0, 1)]
    ahead = along_z(jnp.stack([unit[size : 2 * size] for unit in units]), {0: 2, 1: 3})
    units = [jnp.where(z < 2, unit[:size], later) for unit, later in zip(units, ahead)]
    rows = [pick(owner, own_rows, other_rows) for owner in (0, 1)]
    return jnp.concatenate([units[0], rows[0], units[1]], axis=0), rows[1]


def fetch(places, gathered_refs, blocks, sems):
    copies, done = [], 0
    for i, ((first, rows), ref) in enumerate(zip(places, gathered_refs)):
        for p in range(16):
            target = blocks.at[p, pl.ds(done, rows)]
            copies.append(pltpu.make_async_copy(ref.at[p, pl.ds(first, rows)], target, sems.at[16 * i + p]))
        done += rows
    for copy in copies:
        copy.start()
    return copies


def unit_weights_kernel(section, places, gathered_ref, _, *refs):
    *out_refs, gain_ref, blocks, wide, sems = refs
    for copy in fetch(places, [gathered_ref], blocks, sems):
        copy.wait()
    owner = section // 2
    gain_ref[...] = blocks[spot(owner, 0, 0), UNIT : UNIT + GAIN, :]
    q_ref, k_ref, v_ref, o_ref = out_refs
    for k in range(4):
        block = lambda d, low, high: blocks[spot(k % 2, d // 2 + 2 * (k // 2), d % 2), low:high, :]
        lanes = slice(128 * k, 128 * k + 128)
        far = slice(512 + 128 * k, 512 + 128 * k + 128)
        if section:
            q_ref[:, lanes] = block(0, 0, 1024)
            k_ref[:, lanes] = block(1, 0, 1024)
            v_ref[:, lanes] = block(2, 0, 1024)
            o_ref[:, lanes] = block(3, 0, 512)
            o_ref[:, far] = block(3, 512, 1024)
        else:
            wide[0, pl.ds(k, 256, stride=4), :] = block(0, 0, 256).astype(f32)
            wide[1, pl.ds(k, 256, stride=4), :] = block(0, 256, 512).astype(f32)
            v_ref[:512, lanes] = block(0, 512, 1024)
            v_ref[512:, lanes] = block(1, 0, 512)
            o_ref[:, lanes] = block(2, 0, 512)
            o_ref[:, far] = block(2, 512, 1024)
    if section == 0:
        q_ref[...] = wide[0].astype(bf16)
        k_ref[...] = wide[1].astype(bf16)


def unit_weights(section, earlier, places, *gathered):
    narrow = (D, 512 if section else 128)
    shapes = [narrow, narrow, (D, 512), (512, D), (GAIN, TILE)]
    *weights, gain = pl.pallas_call(
        partial(unit_weights_kernel, section, places),
        in_specs=[pl.BlockSpec(memory_space=pltpu.HBM), pl.BlockSpec(memory_space=pl.ANY)],
        out_shape=[jax.ShapeDtypeStruct(shape, bf16) for shape in shapes],
        scratch_shapes=[
            pltpu.VMEM((16, UNIT + GAIN, TILE), bf16),
            pltpu.VMEM((2, 1024, TILE), f32),
            pltpu.SemaphoreType.DMA((16,)),
        ],
        compiler_params=pltpu.CompilerParams(vmem_limit_bytes=40 * 2**20),
    )(*gathered, earlier)
    return gain[:8].reshape(1, D).astype(f32), tuple(weights)


def row_places():
    places = []
    for d in range(6):
        for part, count, skipped in ((0, 17 if d < 5 else 6, 0), (1, 16 if d < 5 else 5, 17 if d < 5 else 6)):
            places.append((spot(part, d // 2, d % 2), 33 * d + skipped, count))
    return places


def strip_places():
    places = [(spot(part, 2, 1), (6, 5)[part] * TILE, 176, 176 * part, 176) for part in (0, 1)]
    for i in range(4):
        places.append((spot(i % 2, 3, i // 2), 0, 272, 352 + 264 * i, 264))
    return places


def row_weights_kernel(section, places, *refs):
    gathered_refs = refs[: len(places)]
    gate_ref, up_ref, down_ref, gain_ref, blocks, wide, sems = refs[len(places) + 1 :]
    for copy in fetch(places, gathered_refs, blocks, sems):
        copy.wait()
    gain_ref[...] = blocks[spot(section // 2, 0, 0), ROWS : ROWS + GAIN, :]
    for p, start, count in row_places():
        for i in range(count):
            r, j = (start + i) // 11, (start + i) % 11
            ref = gate_ref if r < 8 else up_ref
            ref[TILE * (r % 8) : TILE * (r % 8) + TILE, TILE * j : TILE * j + TILE] = blocks[
                p, TILE * i : TILE * i + TILE, :
            ]
    for p, start, step, unit, count in strip_places():
        for j in range(8):
            value = blocks[p, start + step * j : start + step * j + step, :].astype(f32)
            wide[unit : unit + count, TILE * j : TILE * j + TILE] = value[:count]
    down_ref[...] = wide[...].astype(bf16)


def row_weights(section, earlier, places, *gathered):
    shapes = [(D, WIDE), (D, WIDE), (WIDE, D), (GAIN, TILE)]
    *weights, gain = pl.pallas_call(
        partial(row_weights_kernel, section, places),
        in_specs=[pl.BlockSpec(memory_space=pltpu.HBM)] * len(places) + [pl.BlockSpec(memory_space=pl.ANY)],
        out_shape=[jax.ShapeDtypeStruct(shape, bf16) for shape in shapes],
        scratch_shapes=[
            pltpu.VMEM((16, ROWS + GAIN, TILE), bf16),
            pltpu.VMEM((WIDE, D), f32),
            pltpu.SemaphoreType.DMA((16 * len(places),)),
        ],
        compiler_params=pltpu.CompilerParams(vmem_limit_bytes=48 * 2**20),
    )(*gathered, earlier)
    return gain[:8].reshape(1, D).astype(f32), tuple(weights)


def halves_of(refs):
    if len(refs) == 2:
        return refs
    rows = refs[0].shape[0] // 2
    return refs[0].at[:rows], refs[0].at[rows:]


def dot_rows(first, lanes, second):
    return sum(dot_tn(a[:, lanes], b[...]) for a, b in zip(first, second))


def grouped(counts, refs):
    groups, at = [], 0
    for count in counts:
        group = refs[at : at + count]
        groups.append(group if len(set(counts)) == 1 else halves_of(group))
        at += count
    return groups, refs[at:]


def pack_rows_kernel(counts, *refs):
    (hidden, gate, up, activ, grad), refs = grouped(counts, refs)
    _, out_ref, done_ref, wide = refs
    done_ref[...] = jnp.zeros_like(done_ref)
    place_of = {}
    for p, start, count in row_places():
        for i in range(count):
            place_of[start + i] = (p, i)
    for side, local in enumerate((gate, up)):
        for first in (0, 512):
            value = dot_rows(hidden, slice(first, first + 512), local).astype(bf16)
            for r in range(4):
                for j in range(11):
                    p, i = place_of[11 * (8 * side + first // TILE + r) + j]
                    out_ref[p, TILE * i : TILE * i + TILE, :] = value[
                        TILE * r : TILE * r + TILE, TILE * j : TILE * j + TILE
                    ]
    for first, count in ((0, 512), (512, 512), (1024, 384)):
        wide[first : first + count, :] = dot_rows(activ, slice(first, first + count), grad)
    wide[WIDE:, :] = jnp.zeros((8, D), f32)
    for p, start, step, unit, _ in strip_places():
        for j in range(8):
            value = wide[unit : unit + step, TILE * j : TILE * j + TILE].astype(bf16)
            out_ref[p, start + step * j : start + step * j + step, :] = value


def pack_rows(hidden, grad_gate, grad_up, activ, grad, earlier):
    operands = (hidden, grad_gate, grad_up, activ, grad)
    counts = [len(operand) for operand in operands]
    return pl.pallas_call(
        partial(pack_rows_kernel, counts),
        in_specs=[pl.BlockSpec(memory_space=pltpu.VMEM)] * sum(counts) + [pl.BlockSpec(memory_space=pl.ANY)],
        out_shape=[jax.ShapeDtypeStruct((16, ROWS, TILE), bf16), jax.ShapeDtypeStruct((8, TILE), f32)],
        scratch_shapes=[pltpu.VMEM((WIDE + 8, D), f32)],
        compiler_params=pltpu.CompilerParams(vmem_limit_bytes=48 * 2**20),
        cost_estimate=pl.CostEstimate(flops=2 * 512 * 3 * D * WIDE, bytes_accessed=2**24, transcendentals=0),
    )(*sum(map(list, operands), []), earlier)


def pack_units_kernel(section, counts, info_ref, *refs):
    y, z, c = info_ref[0], info_ref[1], info_ref[2]
    (hidden, grad, gq, gk, gv, mixed), refs = grouped(counts, refs)
    _, out_ref, done_ref, *scratch = refs
    done_ref[...] = jnp.zeros_like(done_ref)

    def store(d, k, low, high, value):
        base = UNIT * (k // 2)
        out_ref[c ^ (d % 2), y ^ (k % 2), (d // 2) ^ (z & 1), base + low : base + high, :] = value

    if section:
        for d, local in enumerate((gq, gk, gv)):
            for r in range(4):
                value = dot_rows(hidden, slice(256 * r, 256 * r + 256), local).astype(bf16)
                for k in range(4):
                    store(d, k, 256 * r, 256 * r + 256, value[:, 128 * k : 128 * k + 128])
        out_d = 3
    else:
        (wide,) = scratch
        for d, local in enumerate((gq, gk)):
            for r in range(4):
                wide[d, 256 * r : 256 * r + 256, :] = dot_rows(hidden, slice(256 * r, 256 * r + 256), local)
            for k in range(4):
                store(0, k, 256 * d, 256 * d + 256, wide[d, pl.ds(k, 256, stride=4), :].astype(bf16))
        for r in range(4):
            value = dot_rows(hidden, slice(256 * r, 256 * r + 256), gv).astype(bf16)
            for k in range(4):
                low = (512, 768, 0, 256)[r]
                store(0 if r < 2 else 1, k, low, low + 256, value[:, 128 * k : 128 * k + 128])
        for k in range(4):
            store(1, k, 512, 1024, jnp.zeros((512, TILE), bf16))
            store(3, k, 0, 1024, jnp.zeros((1024, TILE), bf16))
        out_d = 2
    for r in range(2):
        value = dot_rows(mixed, slice(256 * r, 256 * r + 256), grad).astype(bf16)
        for k in range(8):
            low = 512 * (k // 4) + 256 * r
            store(out_d, k % 4, low, low + 256, value[:, 128 * k : 128 * k + 128])


def pack_units(section, place, hidden, gq, gk, gv, mixed, grad, earlier):
    operands = (hidden, grad, [gq], [gk], [gv], [mixed])
    counts = [len(operand) for operand in operands]
    return pl.pallas_call(
        partial(pack_units_kernel, section, counts),
        in_specs=[pl.BlockSpec(memory_space=pltpu.SMEM)]
        + [pl.BlockSpec(memory_space=pltpu.VMEM)] * sum(counts)
        + [pl.BlockSpec(memory_space=pl.ANY)],
        out_shape=[jax.ShapeDtypeStruct((2, 2, 2, 2 * UNIT, TILE), bf16), jax.ShapeDtypeStruct((8, TILE), f32)],
        scratch_shapes=[] if section else [pltpu.VMEM((2, UNIT, TILE), f32)],
        compiler_params=pltpu.CompilerParams(vmem_limit_bytes=40 * 2**20),
        cost_estimate=pl.CostEstimate(flops=2 * 512 * 4 * D * 512, bytes_accessed=2**23, transcendentals=0),
    )(place, *sum(map(list, operands), []), earlier)


def add(first, second):
    return (first.astype(f32) + second.astype(f32)).astype(bf16)


def scattered(blocks):
    return lax.psum_scatter(blocks, GROUP, scatter_dimension=0, tiled=False)


def param_shard(units, rows, gain, place_rows, received, y, x, z, c, d):
    pick = lambda owner, pair: jnp.where(y == owner, pair[0], pair[1])
    units = [padded(unit, ROWS) for unit in units]
    own_units, other_units = pick(0, units), pick(1, units)
    own_rows, other_rows = pick(0, rows), pick(1, rows)
    from_x = swap_x(jnp.where(x == 0, own_rows, own_units))
    from_xy = swap_xy(jnp.where(x == 0, other_rows, other_units))
    from_y = swap_y(jnp.where(x == 0, other_units, other_rows))
    from_x, gain, *sent, got_out, got_grad = tied(from_x, gain, own_units, other_units, *received)
    results = place_rows((got_out, got_grad))
    gain = gain + along_z(gain, {0: 2, 2: 0, 1: 3, 3: 1})
    gain_own = lax.dynamic_index_in_dim(gain, 2 * y + x, 0, keepdims=True)
    own = jnp.where(x == 0, own_units, own_rows)
    moved = [
        route(block, lambda yy, xx, zz, cc: (0, 0, 0, 1) if (yy, xx, zz, cc) == (source, 0, 1, 0) else None)
        for source, block in enumerate(sent)
    ]
    lined = pl.pallas_call(
        line_kernel,
        in_specs=[pl.BlockSpec(memory_space=pltpu.SMEM)]
        + [pl.BlockSpec(memory_space=pltpu.VMEM)] * 6
        + [pl.BlockSpec(memory_space=pl.ANY)] * 2,
        out_shape=jax.ShapeDtypeStruct((LINED + 64, TILE), f32),
        scratch_shapes=[pltpu.VMEM((22, 384, TILE), f32)],
        compiler_params=pltpu.CompilerParams(vmem_limit_bytes=40 * 2**20),
    )(jnp.stack([x, y, d]), own, from_y, from_x, from_xy, *moved, *results)
    left = dp_right(jnp.where(x == 0, lined[8184:8192], lined[LINED - 8 : LINED]))
    right = dp_left(lined[:256])
    left = jnp.where(d == 0, gain_own.reshape(8, 128), left)
    start = jnp.where(x == 0, jnp.minimum(65 * d, 263), d)
    shard = pl.pallas_call(
        flat_kernel,
        in_specs=[pl.BlockSpec(memory_space=pltpu.SMEM)] + [pl.BlockSpec(memory_space=pltpu.VMEM)] * 3,
        out_specs=pl.BlockSpec(memory_space=pl.ANY),
        out_shape=jax.ShapeDtypeStruct((1, SHARD * 128), f32),
        scratch_shapes=[pltpu.VMEM((8528, 128), f32), pltpu.VMEM((SHARD, 128), f32), pltpu.SemaphoreType.DMA],
        compiler_params=pltpu.CompilerParams(vmem_limit_bytes=40 * 2**20),
    )(jnp.stack([start, x]), lined, left, right)
    return results, shard, gain_own


def mlp_grad(weights, kept, grad):
    w_gate, w_up, w_down = weights
    gate, up = kept[3:5]
    grad_activ = dot_right(grad, w_down)
    sig = jax.nn.sigmoid(gate)
    grad_gate = (grad_activ * up * sig * (1.0 + gate * (1.0 - sig))).astype(bf16)
    grad_up = (grad_activ * gate * sig).astype(bf16)
    partial_hidden = dot_right(grad_gate, w_gate) + dot_right(grad_up, w_up)
    return partial_hidden.astype(bf16), (grad_gate, grad_up)


def added(entry, *parts):
    return (entry.astype(f32) + sum(part.astype(f32) for part in parts)).astype(bf16)


def per_row(inputs, cotangent, seq_lengths, flat_params):
    y, x, z, c = (lax.axis_index(axis) for axis in AXES)
    d = 2 * z + c
    seg_ids = segment_ids(lax.dynamic_index_in_dim(seq_lengths, y, 0, keepdims=False)[0], inputs.shape[1])
    block0, block1 = source_blocks(flat_params, y, x, z, c, d)
    first = lax.all_gather(block0, GROUP)
    first, block1 = tied(first, block1)
    second = lax.all_gather(block1, GROUP)
    unit, rows = UNIT + GAIN, ROWS + GAIN
    gathered = [([(0, unit)], first), ([(unit, rows)], first), ([(unit + rows, unit)], first), ([(0, rows)], second)]
    gains, weights, kept, outputs = [None] * 4, [None] * 4, [None] * 4, [None] * 4
    row_half = inputs.shape[1] // 2

    def cut(rows):
        return [rows[:row_half], rows[row_half:]]

    def join(halves):
        return jnp.concatenate(halves, axis=0)

    def open_section(s, earlier):
        gains[s], weights[s] = (unit_weights if s % 2 == 0 else row_weights)(s, earlier, *gathered[s])
        kept[s] = []
        return gains[s]

    def normed_rows(s, entry):
        hidden, normed, inv_root = norm_forward(entry.astype(f32), gains[s])
        kept[s].append((hidden.astype(bf16), normed, inv_root))
        return kept[s][-1][0]

    def heads(s, entry):
        hidden = normed_rows(s, entry)
        return [dot_plain(hidden, w).astype(bf16) for w in weights[s][:3]]

    def attention(s, parts):
        q, k, v = (join(halves) for halves in zip(*parts))
        mixed = mix(s == 0, seg_ids, q, k, v)
        kept[s].append((q, k, v, mixed))
        return [dot_plain(half, weights[s][3]).astype(bf16) for half in cut(mixed)]

    def mlp(s, entry):
        hidden = normed_rows(s, entry)
        w_gate, w_up, _ = weights[s]
        gate = dot_plain(hidden, w_gate)
        up = dot_plain(hidden, w_up)
        activ = (jax.nn.silu(gate) * up).astype(bf16)
        kept[s][-1] += (gate, up, activ)
        return activ

    entry = cut(lax.dynamic_index_in_dim(inputs, y, 0, keepdims=False))
    open_section(0, entry[0])
    branch = attention(0, [heads(0, half) for half in entry])
    got = [swap_x(half) for half in branch]
    open_section(1, branch[0])
    entry[0] = added(entry[0], branch[0], got[0])
    next_branch = [dot_plain(mlp(1, entry[0]), weights[1][2]).astype(bf16)]
    got[1], next_branch[0] = tied(got[1], next_branch[0])
    entry[1] = added(entry[1], branch[1], got[1])
    outputs[0] = list(entry)
    next_branch.append(dot_plain(mlp(1, entry[1]), weights[1][2]).astype(bf16))
    branch = next_branch
    got = [swap_x(half) for half in branch]
    open_section(2, branch[1])
    entry[0] = added(entry[0], branch[0], got[0])
    first_heads = heads(2, entry[0])
    got[1], first_heads[0] = tied(got[1], first_heads[0])
    entry[1] = added(entry[1], branch[1], got[1])
    outputs[1] = list(entry)
    branch = join(attention(2, [first_heads, heads(2, entry[1])]))
    got = swap_x(branch)
    done = open_section(3, branch)
    got, _ = tied(got, done)

    grads, gain_sums, sums = [None] * 4, [0.0] * 4, [None] * 4
    place = jnp.stack([y, z, c])

    def finish(s, half, grad, part, got):
        grad_hidden = part.astype(f32) + got.astype(f32)
        _, normed, inv_root = kept[s][half][:3]
        grad_entry, grad_gain = norm_backward(grad_hidden, gains[s], normed, inv_root)
        gain_sums[s] += grad_gain
        return (grad.astype(f32) + grad_entry).astype(bf16)

    def finish_rows(s, grad, parts, got):
        return [finish(s, half, *rows) for half, rows in enumerate(zip(grad, parts, cut(got)))]

    def pack_mlp(s, local, grad, earlier):
        hidden = [half[0] for half in kept[s]]
        activ = [half[5] for half in kept[s]]
        return pack_rows(hidden, *([half[i] for half in local] for i in (0, 1)), activ, grad, earlier)

    def mix_parts(s, grad_mixed):
        q, k, v, mixed = kept[s][2]
        local = mix_grad(s == 0, seg_ids, q, k, v, join(grad_mixed))
        w_query, w_key, w_value, _ = weights[s]
        parts = []
        for gq, gk, gv in zip(*(cut(part) for part in local)):
            parts.append((dot_right(gq, w_query) + dot_right(gk, w_key) + dot_right(gv, w_value)).astype(bf16))
        return parts, local

    def pack_attention(s, local, grad, earlier):
        hidden = [half[0] for half in kept[s][:2]]
        return pack_units(s, place, hidden, *local, kept[s][2][3], grad, earlier)

    def near(value):
        return along_z(value, {0: 1, 1: 0, 2: 3, 3: 2})

    def far(value):
        return along_z(value, {2: 0, 3: 1})

    grad = lax.dynamic_index_in_dim(cotangent, y, 0, keepdims=False)
    entry = added(join(entry), branch, got)
    outputs[2] = [entry]
    branch = dot_plain(mlp(3, entry), weights[3][2]).astype(bf16)
    part, local = mlp_grad(weights[3], kept[3][0], grad)
    got = swap_x(part)
    packed, done = pack_mlp(3, [local], [grad], part)
    sums[3] = scattered(packed)
    got, _, branch = tied(got, done, branch)
    grad = finish(3, 0, grad, part, got)
    grads[3] = [grad]

    parts, local = mix_parts(2, [dot_right(grad, weights[2][3]).astype(bf16)])
    part, got_out = tied(join(parts), swap_x(branch))
    outputs[3] = [added(entry, branch, got_out)]
    got = swap_x(part)
    packed, done = pack_attention(2, local, [grad], part)
    got, _ = tied(got, done)
    grad = grads[2] = finish_rows(2, cut(grad), cut(part), got)
    parts2 = add(packed[0], swap_c(packed[1]))

    parts, local = zip(*(mlp_grad(weights[1], kept[1][half], grad[half]) for half in range(2)))
    part = join(parts)
    got = swap_x(part)
    packed, done = pack_mlp(1, local, grad, part)
    sums[1] = scattered(packed)
    got, _, got_y = tied(got, done, swap_y(parts2[1]))
    grad = grads[1] = finish_rows(1, grad, cut(part), got)
    parts2 = add(parts2[0], got_y)

    parts, local = mix_parts(0, [dot_right(half, weights[0][3]).astype(bf16) for half in grad])
    part = join(parts)
    got = swap_x(part)
    packed, _ = pack_attention(0, local, grad, part)
    parts0 = add(packed[0], swap_c(packed[1]))
    outputs = [join(halves) for halves in outputs]
    sent = by_index(2 * (1 - y) + x, outputs)
    got, got_y, got_z, sent = tied(got, swap_y(parts0[1]), near(parts2[1]), sent)
    parts0, parts2 = add(parts0[0], got_y), add(parts2[0], got_z)
    grads[0] = finish_rows(0, grad, cut(part), got)
    grads = [join(halves) for halves in grads]

    got_z, got_far = near(parts0[1]), far(parts2)
    gain = jnp.concatenate(gain_sums, axis=0)
    gain = gain + swap_c(gain)
    got_gain, sent, grad_sent = tied(swap_y(gain), sent, by_index(2 * (1 - y) + x, grads))
    got_out, got_grad = swap_y(sent), swap_y(grad_sent)
    gain, parts0 = gain + got_gain, add(parts0[0], got_z)
    gain, sums[0], sums[2] = gain + near(gain), add(parts0, far(parts0)), add(parts2, got_far)

    def place_rows(received):
        placed = []
        for rows_of, got in zip((outputs, grads), received):
            own = by_index(2 * y + x, rows_of)
            placed.append(jnp.stack([jnp.where(y == 0, own, got), jnp.where(y == 0, got, own)])[None])
        return placed

    results, shard, gain_own = param_shard(
        (sums[0], sums[2]), (sums[1], sums[3]), gain, place_rows, (got_out, got_grad), y, x, z, c, d
    )
    return *results, shard, gain_own


def solution(mesh):
    if mesh.shape["section"] == 4 and mesh.shape["dp"] == 2 * DEPTH:
        grid = jax.sharding.Mesh(mesh.devices.reshape(2, 2, DEPTH, 2), AXES)
        function, section, dp = per_row, ("y", "x"), ("z", "c")
    else:
        grid, function, section, dp = mesh, per_device, "section", "dp"
    return jax.shard_map(
        function,
        mesh=grid,
        in_specs=(P(None, dp, None), P(None, dp, None), P(None, dp, None), P(section, dp)),
        out_specs=(P(section, None, dp, None), P(section, None, dp, None), P(section, dp), P(section, None)),
        check_vma=False,
    )
```

```python
from functools import partial

import jax
import jax.numpy as jnp
import numpy as np
from jax import lax
from jax.experimental import pallas as pl
from jax.experimental.pallas import tpu as pltpu
from jax.sharding import PartitionSpec as P

D = 1024
FF = 2752
HEADS = 16
FEAT = 16
WINDOW = 64


EPS = 1e-05
NEG_LARGE = -1e30


def shortened(x):

    def short(part):
        return part.astype(jnp.bfloat16) if part.dtype == jnp.float32 else part

    return jax.tree.map(short, x)


def passed_along(value, axis, steps):
    count = lax.axis_size(axis)
    initial, last = (max(0, -steps), min(count, count - steps))
    return lax.ppermute(value, axis, [(source, source + steps) for source in range(initial, last)])


def layout(section_kind):
    if section_kind == 0:
        return [(1, D), (D, HEADS * FEAT), (D, HEADS * FEAT), (D, D), (D, D)]
    if section_kind == 2:
        return [(1, D), (D, D), (D, D), (D, D), (D, D)]
    return [(1, D), (D, FF), (D, FF), (FF, D)]


def unpack(flat_vec, section_kind):
    pieces = []
    offset = 0
    for row_count, col_count in layout(section_kind):
        pieces.append(
            flat_vec[offset : offset + row_count * col_count].reshape(row_count, col_count)
        )
        offset += row_count * col_count
    return pieces


def flatten_grads(grad_pieces, total_size):
    joined = jnp.concatenate([grad_piece.reshape(-1) for grad_piece in grad_pieces])
    return jnp.pad(joined, (0, total_size - joined.shape[0]))


def dot_plain(first_op, second_op):
    return jnp.dot(first_op, second_op, preferred_element_type=jnp.float32)


def dot_left(first_op, second_op):
    return lax.dot_general(
        first_op, second_op, (((0,), (0,)), ((), ())), preferred_element_type=jnp.float32
    )


def dot_right(first_op, second_op):
    return lax.dot_general(
        first_op, second_op, (((1,), (1,)), ((), ())), preferred_element_type=jnp.float32
    )


def segment_ids(lengths_row, total_rows):
    doc_ends = jnp.cumsum(lengths_row)
    positions = jnp.arange(total_rows, dtype=jnp.int32)
    return jnp.sum((positions[:, None] >= doc_ends[None, :]).astype(jnp.int32), axis=1)


def norm_forward(entry_val, gain_f32):
    inv_root = lax.rsqrt(jnp.mean(entry_val * entry_val, axis=-1, keepdims=True) + EPS)
    normed = entry_val * inv_root
    return (normed * gain_f32, normed, inv_root)


def norm_backward(grad_hidden, gain_f32, normed, inv_root):
    grad_normed = grad_hidden * gain_f32
    grad_gain = jnp.sum(grad_hidden * normed, axis=0, keepdims=True)
    grad_entry = inv_root * (
        grad_normed - normed * jnp.mean(grad_normed * normed, axis=-1, keepdims=True)
    )
    return (grad_entry, grad_gain)


def block_weights(section_kind, query_rows, key_row_block, seg_ids, start_row_index, block_size):
    final_row_index = start_row_index + block_size
    first_key = 0 if section_kind == 0 else max(0, start_row_index - WINDOW)
    score_scaling_factor = 0.25 if section_kind == 0 else 0.125
    score_matrix = (
        jnp.einsum(
            "ezl,jzl->zej",
            query_rows[start_row_index:final_row_index],
            key_row_block[first_key:final_row_index],
            preferred_element_type=jnp.float32,
        )
        * score_scaling_factor
    )
    query_pos = start_row_index + jnp.arange(block_size, dtype=jnp.int32)
    key_pos = first_key + jnp.arange(final_row_index - first_key, dtype=jnp.int32)
    allowed = (key_pos[None, :] <= query_pos[:, None]) & (
        seg_ids[first_key:final_row_index][None, :]
        == seg_ids[start_row_index:final_row_index][:, None]
    )
    if section_kind == 0:
        weights = jnp.where(
            allowed[None], 1.0 + score_matrix + 0.5 * score_matrix * score_matrix, 0.0
        )
        totals = jnp.sum(weights, axis=-1, keepdims=True)
        return (score_matrix, allowed, weights / totals, totals, first_key)
    allowed = allowed & (query_pos[:, None] - key_pos[None, :] < WINDOW)
    masked = jnp.where(allowed[None], score_matrix, NEG_LARGE)
    exponent = jnp.where(
        allowed[None], jnp.exp(masked - jnp.max(masked, axis=-1, keepdims=True)), 0.0
    )
    totals = jnp.sum(exponent, axis=-1, keepdims=True)
    return (score_matrix, allowed, exponent / totals, totals, first_key)


def mix_forward(section_kind, query_rows, key_row_block, values, seg_ids):
    row_total = query_rows.shape[0]
    block_size = min(512, row_total)
    outputs = []
    for start_row_index in range(0, row_total, block_size):
        score_matrix, allowed, soft_weights, totals, first_key = block_weights(
            section_kind, query_rows, key_row_block, seg_ids, start_row_index, block_size
        )
        outputs.append(
            jnp.einsum(
                "hqk,khv->qhv",
                soft_weights.astype(jnp.bfloat16),
                values[first_key : start_row_index + block_size],
                preferred_element_type=jnp.float32,
            )
        )
    return jnp.concatenate(outputs, axis=0).astype(jnp.bfloat16)


def mix_backward(section_kind, query_rows, key_row_block, values, seg_ids, grad_mixed):
    row_total = query_rows.shape[0]
    block_size = min(512, row_total)
    score_scaling_factor = 0.25 if section_kind == 0 else 0.125
    grad_query_parts = []
    mixed_parts = []
    grad_keys = jnp.zeros(key_row_block.shape, jnp.float32)
    grad_values = jnp.zeros(values.shape, jnp.float32)
    for start_row_index in range(0, row_total, block_size):
        final_row_index = start_row_index + block_size
        score_matrix, allowed, soft_weights, totals, first_key = block_weights(
            section_kind, query_rows, key_row_block, seg_ids, start_row_index, block_size
        )
        rounded_weights = soft_weights.astype(jnp.bfloat16)
        value_block = values[first_key:final_row_index]
        grad_block = grad_mixed[start_row_index:final_row_index]
        mixed_parts.append(
            jnp.einsum(
                "hqk,khv->qhv", rounded_weights, value_block, preferred_element_type=jnp.float32
            )
        )
        grad_values = grad_values.at[first_key:final_row_index].add(
            jnp.einsum(
                "hqk,qhv->khv", rounded_weights, grad_block, preferred_element_type=jnp.float32
            )
        )
        grad_weights = jnp.einsum(
            "qhv,khv->hqk", grad_block, value_block, preferred_element_type=jnp.float32
        )
        centred = grad_weights - jnp.sum(grad_weights * soft_weights, axis=-1, keepdims=True)
        if section_kind == 0:
            grad_scores = jnp.where(allowed[None], centred * (1.0 + score_matrix) / totals, 0.0)
        else:
            grad_scores = jnp.where(allowed[None], soft_weights * centred, 0.0)
        grad_scores = grad_scores.astype(jnp.bfloat16)
        grad_query_parts.append(
            jnp.einsum(
                "ncw,wne->cne",
                grad_scores,
                key_row_block[first_key:final_row_index],
                preferred_element_type=jnp.float32,
            )
            * score_scaling_factor
        )
        grad_keys = grad_keys.at[first_key:final_row_index].add(
            jnp.einsum(
                "zas,aze->sze",
                grad_scores,
                query_rows[start_row_index:final_row_index],
                preferred_element_type=jnp.float32,
            )
            * score_scaling_factor
        )
    mixed_out = jnp.concatenate(mixed_parts, axis=0).astype(jnp.bfloat16)
    grad_query = jnp.concatenate(grad_query_parts, axis=0).astype(jnp.bfloat16)
    return (mixed_out, grad_query, grad_keys.astype(jnp.bfloat16), grad_values.astype(jnp.bfloat16))


def attention_setup(flat_vec, residual, section_kind):
    norm_gain, w_query, w_key, w_value, w_out = unpack(flat_vec, section_kind)
    entry_val = residual.astype(jnp.float32)
    gain_f32 = norm_gain.astype(jnp.float32)
    normed_out, normed, inv_root = norm_forward(entry_val, gain_f32)
    hidden = normed_out.astype(jnp.bfloat16)
    row_total = residual.shape[0]
    query_rows = dot_plain(hidden, w_query).astype(jnp.bfloat16).reshape(row_total, HEADS, -1)
    key_row_block = dot_plain(hidden, w_key).astype(jnp.bfloat16).reshape(row_total, HEADS, -1)
    values = dot_plain(hidden, w_value).astype(jnp.bfloat16).reshape(row_total, HEADS, -1)
    return (
        w_query,
        w_key,
        w_value,
        w_out,
        entry_val,
        gain_f32,
        normed,
        inv_root,
        hidden,
        query_rows,
        key_row_block,
        values,
    )


def attention_forward(flat_vec, residual, seg_ids, section_kind):
    (
        w_query,
        w_key,
        w_value,
        w_out,
        entry_val,
        gain_f32,
        normed,
        inv_root,
        hidden,
        query_rows,
        key_row_block,
        values,
    ) = attention_setup(flat_vec, residual, section_kind)
    mixed_out = mix_forward(section_kind, query_rows, key_row_block, values, seg_ids)
    branch_out = dot_plain(mixed_out.reshape(residual.shape[0], -1), w_out)
    return (entry_val + branch_out).astype(jnp.bfloat16)


def attention_backward(flat_vec, residual, seg_ids, grad_out, section_kind):
    (
        w_query,
        w_key,
        w_value,
        w_out,
        entry_val,
        gain_f32,
        normed,
        inv_root,
        hidden,
        query_rows,
        key_row_block,
        values,
    ) = attention_setup(flat_vec, residual, section_kind)
    row_total = residual.shape[0]
    grad_mixed = dot_right(grad_out, w_out).astype(jnp.bfloat16).reshape(row_total, HEADS, -1)
    mixed_out, grad_query, grad_keys, grad_values = mix_backward(
        section_kind, query_rows, key_row_block, values, seg_ids, grad_mixed
    )
    grad_w_out = dot_left(mixed_out.reshape(row_total, -1), grad_out)
    grad_query = grad_query.reshape(row_total, -1)
    grad_keys = grad_keys.reshape(row_total, -1)
    grad_values = grad_values.reshape(row_total, -1)
    grad_hidden = (
        dot_right(grad_query, w_query)
        + dot_right(grad_keys, w_key)
        + dot_right(grad_values, w_value)
    )
    grad_entry, grad_gain = norm_backward(grad_hidden, gain_f32, normed, inv_root)
    grad_in = (grad_out.astype(jnp.float32) + grad_entry).astype(jnp.bfloat16)
    grad_flat = flatten_grads(
        [
            grad_gain,
            dot_left(hidden, grad_query),
            dot_left(hidden, grad_keys),
            dot_left(hidden, grad_values),
            grad_w_out,
        ],
        flat_vec.shape[0],
    )
    return (grad_in, grad_flat)


def mlp_setup(flat_vec, residual):
    norm_gain, w_gate, w_up, w_down = unpack(flat_vec, 1)
    entry_val = residual.astype(jnp.float32)
    gain_f32 = norm_gain.astype(jnp.float32)
    normed_out, normed, inv_root = norm_forward(entry_val, gain_f32)
    hidden = normed_out.astype(jnp.bfloat16)
    gate_pre = dot_plain(hidden, w_gate)
    up_pre = dot_plain(hidden, w_up)
    return (w_gate, w_up, w_down, entry_val, gain_f32, normed, inv_root, hidden, gate_pre, up_pre)


def mlp_forward(flat_vec, residual, seg_ids):
    w_gate, w_up, w_down, entry_val, gain_f32, normed, inv_root, hidden, gate_pre, up_pre = (
        mlp_setup(flat_vec, residual)
    )
    activation = (jax.nn.silu(gate_pre) * up_pre).astype(jnp.bfloat16)
    return (entry_val + dot_plain(activation, w_down)).astype(jnp.bfloat16)


def mlp_backward(flat_vec, residual, seg_ids, grad_out):
    w_gate, w_up, w_down, entry_val, gain_f32, normed, inv_root, hidden, gate_pre, up_pre = (
        mlp_setup(flat_vec, residual)
    )
    sigmoid_gate = jax.nn.sigmoid(gate_pre)
    silu_gate = gate_pre * sigmoid_gate
    activation = (silu_gate * up_pre).astype(jnp.bfloat16)
    grad_w_down = dot_left(activation, grad_out)
    grad_activation = dot_right(grad_out, w_down)
    grad_gate = (
        grad_activation * up_pre * sigmoid_gate * (1.0 + gate_pre * (1.0 - sigmoid_gate))
    ).astype(jnp.bfloat16)
    grad_up = (grad_activation * silu_gate).astype(jnp.bfloat16)
    grad_hidden = dot_right(grad_gate, w_gate) + dot_right(grad_up, w_up)
    grad_entry, grad_gain = norm_backward(grad_hidden, gain_f32, normed, inv_root)
    grad_in = (grad_out.astype(jnp.float32) + grad_entry).astype(jnp.bfloat16)
    grad_flat = flatten_grads(
        [grad_gain, dot_left(hidden, grad_gate), dot_left(hidden, grad_up), grad_w_down],
        flat_vec.shape[0],
    )
    return (grad_in, grad_flat)


def spare_forward(flat_vec, residual, seg_ids):
    return jnp.zeros_like(residual)


def spare_backward(flat_vec, residual, seg_ids, grad_out):
    return (jnp.zeros_like(residual), jnp.zeros(flat_vec.shape, jnp.float32))


def store_slot(buffer, new_value, slot_index, active):
    current = lax.dynamic_index_in_dim(buffer, slot_index, 0, keepdims=False)
    return lax.dynamic_update_slice_in_dim(
        buffer, jnp.where(active, new_value, current)[None], slot_index, 0
    )


def per_device(inputs, cotangent, seq_lengths, flat_params):
    section_now = lax.axis_index("section")
    section_count = lax.axis_size("section")
    micro_count = inputs.shape[0]
    row_total = inputs.shape[1]
    shard_low = flat_params.astype(jnp.bfloat16)
    gathered = lax.all_gather(shard_low, "dp", axis=1, tiled=True)[0]
    forward_fns = [
        partial(attention_forward, section_kind=0),
        mlp_forward,
        partial(attention_forward, section_kind=2),
        mlp_forward,
        spare_forward,
    ]
    backward_fns = [
        partial(attention_backward, section_kind=0),
        mlp_backward,
        partial(attention_backward, section_kind=2),
        mlp_backward,
        spare_backward,
    ]
    saved_inputs = jnp.zeros_like(inputs)
    produced = jnp.zeros_like(inputs)
    previous = jnp.zeros(inputs.shape[1:], jnp.bfloat16)
    for tick_step in range(micro_count + section_count - 1):
        micro_index = tick_step - section_now
        active = (micro_index >= 0) & (micro_index < micro_count)
        chosen = jnp.clip(micro_index, 0, micro_count - 1)
        if tick_step > 0:
            arrived = jax.tree.map(
                lambda part, own: part.astype(own.dtype),
                passed_along(shortened(previous), "section", 1),
                previous,
            )
        else:
            arrived = previous
        residual = jnp.where(
            section_now == 0, lax.dynamic_index_in_dim(inputs, chosen, 0, keepdims=False), arrived
        )
        lengths_row = lax.dynamic_index_in_dim(seq_lengths, chosen, 0, keepdims=False)[0]
        seg_ids = segment_ids(lengths_row, row_total)
        branch_index = jnp.where(active, section_now, 4)
        result = lax.switch(branch_index, forward_fns, gathered, residual, seg_ids)
        saved_inputs = store_slot(saved_inputs, residual, chosen, active)
        produced = store_slot(produced, result, chosen, active)
        previous = result
    back_weights = lax.all_gather(shard_low, "dp", axis=1, tiled=True)[0]
    grads_in = jnp.zeros_like(inputs)
    grad_total = jnp.zeros(gathered.shape, jnp.float32)
    gain_total = jnp.zeros((D,), jnp.float32)
    previous_grad = jnp.zeros(inputs.shape[1:], jnp.bfloat16)
    for tick_step in range(micro_count + section_count - 1):
        micro_index = micro_count - 1 - tick_step + (section_count - 1 - section_now)
        active = (micro_index >= 0) & (micro_index < micro_count)
        chosen = jnp.clip(micro_index, 0, micro_count - 1)
        if tick_step > 0:
            arrived = jax.tree.map(
                lambda part, own: part.astype(own.dtype),
                passed_along(shortened(previous_grad), "section", -1),
                previous_grad,
            )
        else:
            arrived = previous_grad
        grad_out = jnp.where(
            section_now == section_count - 1,
            lax.dynamic_index_in_dim(cotangent, chosen, 0, keepdims=False),
            arrived,
        )
        residual = lax.dynamic_index_in_dim(saved_inputs, chosen, 0, keepdims=False)
        lengths_row = lax.dynamic_index_in_dim(seq_lengths, chosen, 0, keepdims=False)[0]
        seg_ids = segment_ids(lengths_row, row_total)
        branch_index = jnp.where(active, section_now, 4)
        grad_in, grad_flat = lax.switch(
            branch_index, backward_fns, back_weights, residual, seg_ids, grad_out
        )
        grads_in = store_slot(grads_in, grad_in, chosen, active)
        gain_total = gain_total + grad_flat[0:D]
        grad_total = grad_total + grad_flat
        previous_grad = grad_in
    shard_total = lax.psum_scatter(grad_total[None], "dp", scatter_dimension=1, tiled=True)
    gain_grads = lax.psum(gain_total, "dp")[None]
    return (produced[None], grads_in[None], shard_total, gain_grads)


AXES = ("y", "x", "z", "c")
GROUP = ("y", "z", "c")
DEPTH = 4
WIDE = 1408
TILE = 128
STRETCHES = ((0, 172, 176), (688, 258, 264), (1720, 258, 264))
bf16 = jnp.bfloat16
f32 = jnp.float32


def unit_columns(half):
    order = []
    for first, count, padded in STRETCHES:
        for part in (2 * half, 2 * half + 1):
            start = first + count * part
            order += list(range(start, start + count)) + [-1] * (padded - count)
    return order


COLUMNS = np.array(unit_columns(0) + unit_columns(1), np.int32)


def route(value, rule):
    pairs = []
    for y in range(2):
        for x in range(2):
            for z in range(DEPTH):
                for c in range(2):
                    target = rule(y, x, z, c)
                    if target is not None:
                        ty, tx, tz, tc = target
                        pairs.append((((2 * y + x) * DEPTH + z) * 2 + c, ((2 * ty + tx) * DEPTH + tz) * 2 + tc))
    return lax.ppermute(value, AXES, pairs)


def swap_x(value):
    return route(value, lambda y, x, z, c: (y, 1 - x, z, c))


def swap_y(value):
    return route(value, lambda y, x, z, c: (1 - y, x, z, c))


def swap_xy(value):
    return route(value, lambda y, x, z, c: (1 - y, 1 - x, z, c))


def swap_c(value):
    return route(value, lambda y, x, z, c: (y, x, z, 1 - c))


def along_z(value, moves):
    return route(value, lambda y, x, z, c: (y, x, moves[z], c) if z in moves else None)


def spot(y, z, c):
    return (y * DEPTH + z) * 2 + c


def by_index(index, choices):
    result = choices[-1]
    for i in range(len(choices) - 2, -1, -1):
        result = jnp.where(index == i, choices[i], result)
    return result


def tied(*values):
    spec = pl.BlockSpec(memory_space=pl.ANY)
    return pl.pallas_call(
        lambda *refs: None,
        in_specs=[spec] * len(values),
        out_specs=[spec] * len(values),
        out_shape=[jax.ShapeDtypeStruct(value.shape, value.dtype) for value in values],
        input_output_aliases={i: i for i in range(len(values))},
    )(*values)


def lane_mask(width, lanes, index):
    return (lax.broadcasted_iota(jnp.int32, (1, lanes), 1) // width) == index


def dot_nt(a, b):
    return lax.dot_general(a, b, (((1,), (1,)), ((), ())), preferred_element_type=f32)


def dot_tn(a, b):
    return lax.dot_general(a, b, (((0,), (0,)), ((), ())), preferred_element_type=f32)


def pair_mask(row_seg, col_seg, row_start, rows, key_start, keys, window):
    query_pos = row_start + lax.broadcasted_iota(jnp.int32, (rows, keys), 0)
    key_pos = key_start + lax.broadcasted_iota(jnp.int32, (rows, keys), 1)
    allowed = (key_pos <= query_pos) & (
        col_seg[row_start : row_start + rows, :] == row_seg[:, key_start : key_start + keys]
    )
    if window:
        allowed = allowed & (query_pos - key_pos < window)
    return allowed


def tiles(taylor, row_total):
    step = 256
    reach = row_total if taylor else 128
    return [(start, step, max(0, start - reach)) for start in range(0, row_total, step)]


def probabilities(taylor, score, allowed):
    if taylor:
        poly = jnp.where(allowed, 1.0 + score + 0.5 * score * score, 0.0)
        inv_total = 1.0 / jnp.sum(poly, axis=-1, keepdims=True)
        return poly * inv_total, inv_total
    masked = jnp.where(allowed, score, NEG_LARGE)
    expo = jnp.where(allowed, jnp.exp(masked - jnp.max(masked, axis=-1, keepdims=True)), 0.0)
    inv_total = 1.0 / jnp.sum(expo, axis=-1, keepdims=True)
    return expo * inv_total, inv_total


def mix_kernel(taylor, row_seg_ref, col_seg_ref, q_ref, k_ref, v_ref, out_ref):
    row_seg, col_seg = row_seg_ref[...], col_seg_ref[...]
    row_total = q_ref.shape[0]
    for start, rows, first in tiles(taylor, row_total):
        keys = start + rows - first
        allowed = pair_mask(row_seg, col_seg, start, rows, first, keys, 0 if taylor else WINDOW)
        for pair in range(v_ref.shape[1] // 128):
            lanes = slice(128 * pair, 128 * pair + 128)
            narrow = slice(0, 128) if taylor else lanes
            outs = []
            for j in range(2):
                qk_mask = lane_mask(16, 128, 2 * pair + j) if taylor else lane_mask(64, 128, j)
                q = jnp.where(qk_mask, q_ref[start : start + rows, narrow], 0).astype(bf16)
                score = dot_nt(q, k_ref[first : first + keys, narrow]) * (0.25 if taylor else 0.125)
                probs, _ = probabilities(taylor, score, allowed)
                outs.append(
                    jnp.dot(probs.astype(bf16), v_ref[first : first + keys, lanes], preferred_element_type=f32)
                )
            out_ref[start : start + rows, lanes] = jnp.where(lane_mask(64, 128, 0), outs[0], outs[1]).astype(bf16)


def mix_grad_kernel(
    taylor, row_seg_ref, col_seg_ref, q_ref, k_ref, v_ref, gm_ref, gq_ref, gk_ref, gv_ref, aq, ak, av
):
    row_seg, col_seg = row_seg_ref[...], col_seg_ref[...]
    row_total = q_ref.shape[0]
    scale = 0.25 if taylor else 0.125
    aq[...] = jnp.zeros_like(aq)
    ak[...] = jnp.zeros_like(ak)
    av[...] = jnp.zeros_like(av)
    for start, rows, first in tiles(taylor, row_total):
        stop = start + rows
        keys = stop - first
        allowed = pair_mask(row_seg, col_seg, start, rows, first, keys, 0 if taylor else WINDOW)
        for pair in range(v_ref.shape[1] // 128):
            lanes = slice(128 * pair, 128 * pair + 128)
            narrow = slice(0, 128) if taylor else lanes
            for j in range(2):
                qk_mask = lane_mask(16, 128, 2 * pair + j) if taylor else lane_mask(64, 128, j)
                q = jnp.where(qk_mask, q_ref[start:stop, narrow], 0).astype(bf16)
                k = jnp.where(qk_mask, k_ref[first:stop, narrow], 0).astype(bf16)
                gm = jnp.where(lane_mask(64, 128, j), gm_ref[start:stop, lanes], 0).astype(bf16)
                score = dot_nt(q, k) * scale
                probs, inv_total = probabilities(taylor, score, allowed)
                grad_probs = dot_nt(gm, v_ref[first:stop, lanes])
                centred = grad_probs - jnp.sum(grad_probs * probs, axis=-1, keepdims=True)
                if taylor:
                    grad_score = jnp.where(allowed, centred * (1.0 + score) * inv_total, 0.0)
                else:
                    grad_score = probs * centred
                grad_score = grad_score.astype(bf16)
                aq[start:stop, narrow] += jnp.dot(grad_score, k, preferred_element_type=f32) * scale
                ak[first:stop, narrow] += dot_tn(grad_score, q) * scale
                av[first:stop, lanes] += dot_tn(probs.astype(bf16), gm)
    gq_ref[...] = aq[...].astype(bf16)
    gk_ref[...] = ak[...].astype(bf16)
    gv_ref[...] = av[...].astype(bf16)


def mix(taylor, seg_ids, q, k, v):
    return pl.pallas_call(
        partial(mix_kernel, taylor),
        in_specs=[pl.BlockSpec(memory_space=pltpu.VMEM)] * 5,
        out_shape=jax.ShapeDtypeStruct(v.shape, bf16),
        compiler_params=pltpu.CompilerParams(vmem_limit_bytes=32 * 2**20),
        cost_estimate=pl.CostEstimate(flops=2**30, bytes_accessed=2**21, transcendentals=0),
    )(seg_ids[None, :], seg_ids[:, None], q, k, v)


def mix_grad(taylor, seg_ids, q, k, v, gm):
    return pl.pallas_call(
        partial(mix_grad_kernel, taylor),
        in_specs=[pl.BlockSpec(memory_space=pltpu.VMEM)] * 6,
        out_shape=[jax.ShapeDtypeStruct(a.shape, bf16) for a in (q, k, v)],
        scratch_shapes=[pltpu.VMEM(a.shape, f32) for a in (q, k, v)],
        compiler_params=pltpu.CompilerParams(vmem_limit_bytes=32 * 2**20),
        cost_estimate=pl.CostEstimate(flops=3 * 2**30, bytes_accessed=2**22, transcendentals=0),
    )(seg_ids[None, :], seg_ids[:, None], q, k, v, gm)


SHARD = 8257
LINED = 8256
LEFT = 192
UNIT = 1024
ROWS = 2176
GAIN = 16
PAIR = 43


def pieces(position, count, table):
    found = []
    for place in range(count):
        number = int(table[position + place])
        if number < 0:
            continue
        if found and found[-1][1] == place and found[-1][2] + place - found[-1][0] == number:
            found[-1][1] = place + 1
        else:
            found.append([place, place + 1, number])
    return found


def shifted(load, position, last):
    row, shift = position // TILE, position % TILE
    near = load(min(max(row, 0), last))
    if shift == 0:
        return near
    far = load(min(max(row + 1, 0), last))
    lane = lax.broadcasted_iota(jnp.int32, near.shape, 1)
    return pltpu.roll(jnp.where(lane >= shift, near, far), TILE - shift, 1)


def between_lanes(shape, low, high):
    lane = lax.broadcasted_iota(jnp.int32, shape, 1)
    return (lane >= low) & (lane < high)


def masked_rows(value, rows):
    row = lax.broadcasted_iota(jnp.int32, value.shape, 0)
    return jnp.where(row < rows, value, 0.0)


def unit_stretches(owner_y, d, half):
    if owner_y == 1:
        if d == 3:
            return [(512 * half, 0, 1), (512 * half, 4, 1)]
        return [(0, 4 * half, 1), (512, 4 * half, 1)]
    if d == 0:
        return [(0, half, 2), (512, 4 * half, 1)]
    if d == 1:
        return [(0, 4 * half, 1), None]
    return [(0, 0, 1), (0, 4, 1)] if half else [None, None]


UNIT_CASES = [
    (1, 0, lambda y, d: (y == 1) & (d < 3)),
    (1, 3, lambda y, d: (y == 1) & (d == 3)),
    (0, 0, lambda y, d: (y == 0) & (d == 0)),
    (0, 1, lambda y, d: (y == 0) & (d == 1)),
    (0, 2, lambda y, d: (y == 0) & (d == 2)),
]


def source_kernel(info_ref, flat_ref, left_ref, right_ref, out_ref, moved_ref, buf, column, sem):
    copy = pltpu.make_async_copy(flat_ref.reshape(SHARD, TILE), buf.at[pl.ds(LEFT, SHARD)], sem)
    copy.start()
    buf[:LEFT, :] = left_ref[...]
    copy.wait()
    buf[LEFT + SHARD : LEFT + SHARD + 8, :] = right_ref[...]
    start, x, y, d = info_ref[0], info_ref[1], info_ref[2], info_ref[3]
    gain = buf[LEFT : LEFT + GAIN, :].astype(bf16)

    for owner_y, unit_d, chosen in UNIT_CASES:

        @pl.when((x == 0) & chosen(y, d))
        def _(owner_y=owner_y, unit_d=unit_d):
            for half in range(2):
                for k in range(4):
                    part, deep = k % 2, k // 2
                    place, base = half * 2 + (part ^ owner_y), deep * (UNIT + GAIN)
                    for side, stretch in enumerate(unit_stretches(owner_y, unit_d, half)):
                        if stretch is not None:
                            row, strip, step = stretch
                            value = buf[pl.ds(start + 8 * row + strip + step * k, 512, stride=8), :]
                            out_ref[place, base + 512 * side : base + 512 * side + 512, :] = value.astype(bf16)
                    out_ref[place, base + UNIT : base + UNIT + GAIN, :] = gain
            if (owner_y, unit_d) == (0, 1):
                for k in range(4):
                    for side in range(2):
                        value = buf[pl.ds(start + 8 * 512 + 4 * side + k, 512, stride=8), :]
                        row = (k // 2) * (UNIT + GAIN) + 512 * side
                        moved_ref[k % 2, row : row + 512, :] = value.astype(bf16)

    @pl.when((x == 1) & (d <= 5))
    def _():
        for half in range(2):
            for j in range(WIDE // TILE):
                for parity in range(2):
                    load = lambda row: buf[pl.ds(start + row, 192, stride=PAIR), :]
                    value = jnp.zeros((192, TILE), f32)
                    for low, high, number in pieces(WIDE * half + TILE * j, TILE, COLUMNS):
                        got = shifted(load, parity * FF + number - low, PAIR)
                        value = jnp.where(between_lanes(value.shape, low, high), got, value)
                    column[pl.ds(parity, 192, stride=2), :] = value
                whole = column[...].astype(bf16)

                @pl.when(d <= 4)
                def _():
                    for r in range(3):
                        t = 11 * r + j
                        part, place = (0, t) if t < 17 else (1, t - 17)
                        out_ref[(1 - half) * 2 + (y ^ part), TILE * place : TILE * place + TILE, :] = whole[
                            TILE * r : TILE * r + TILE
                        ]

                @pl.when(d == 5)
                def _():
                    part, place = (0, j) if j < 6 else (1, j - 6)
                    out_ref[(1 - half) * 2 + (y ^ part), TILE * place : TILE * place + TILE, :] = whole[:TILE]

    @pl.when(x == 1)
    def _():
        for half in range(2):
            for part in range(2):
                q, place = 2 * half + part, (1 - half) * 2 + (y ^ part)
                out_ref[place, ROWS : ROWS + GAIN, :] = gain

                @pl.when(d == 5)
                def _():
                    for j in range(8):
                        value = buf[pl.ds(start + 8 * (344 + 172 * q) + j, 176, stride=8), :]
                        first = (6, 5)[part] * TILE + 176 * j
                        out_ref[place, first : first + 176, :] = masked_rows(value, 172).astype(bf16)

                @pl.when(d > 5)
                def _():
                    for j in range(8):
                        value = buf[pl.ds(start + 8 * 258 * q + j, 272, stride=8), :]
                        out_ref[place, 272 * j : 272 * j + 272, :] = masked_rows(value, 258).astype(bf16)


def line_kernel(info_ref, *refs):
    block_refs, moved_refs, out_ref, halves = refs[:4], refs[4:6], refs[8], refs[9]
    x, y, d = info_ref[0], info_ref[1], info_ref[2]

    @pl.when(x == 0)
    def _():
        out_ref[...] = jnp.zeros_like(out_ref)

    for owner_y, unit_d, chosen in UNIT_CASES:

        @pl.when((x == 0) & chosen(y, d))
        def _(owner_y=owner_y, unit_d=unit_d):
            for half in range(2):
                for k in range(4):
                    part, deep = k % 2, k // 2
                    ref, base = block_refs[half * 2 + (part ^ owner_y)], UNIT * deep
                    for side, stretch in enumerate(unit_stretches(owner_y, unit_d, half)):
                        if stretch is not None:
                            row, strip, step = stretch
                            value = ref[base + 512 * side : base + 512 * side + 512, :].astype(f32)
                            out_ref[pl.ds(8 * row + strip + step * k, 512, stride=8), :] = value
            if (owner_y, unit_d) == (0, 1):
                for k in range(4):
                    for side in range(2):
                        row = UNIT * (k // 2) + 512 * side
                        value = moved_refs[k % 2][row : row + 512, :].astype(f32)
                        out_ref[pl.ds(8 * 512 + 4 * side + k, 512, stride=8), :] = value

    inverse = np.full((2 * FF,), -1, np.int64)
    for place, number in enumerate(COLUMNS):
        if number >= 0:
            inverse[number] = place
            inverse[FF + number] = 2 * WIDE + place

    for own_y in range(2):

        @pl.when((x == 1) & (d <= 5) & (y == own_y))
        def _(own_y=own_y):
            for half in range(2):
                ref = [block_refs[(1 - half) * 2 + (part ^ own_y)] for part in range(2)]

                @pl.when(d <= 4)
                def _():
                    for t in range(33):
                        part, place = (0, t) if t < 17 else (1, t - 17)
                        r, j = t // 11, t % 11
                        halves[11 * half + j, TILE * r : TILE * r + TILE, :] = ref[part][
                            TILE * place : TILE * place + TILE, :
                        ].astype(f32)

                @pl.when(d == 5)
                def _():
                    for j in range(11):
                        part, place = (0, j) if j < 6 else (1, j - 6)
                        halves[11 * half + j, :TILE, :] = ref[part][
                            TILE * place : TILE * place + TILE, :
                        ].astype(f32)

    @pl.when((x == 1) & (d <= 5))
    def _():
        for b in range(PAIR):
            value = jnp.zeros((192, TILE), f32)
            for low, high, number in pieces(TILE * b, TILE, inverse):
                parity, rest = number // (2 * WIDE), number % (2 * WIDE)
                half, local = rest // WIDE, rest % WIDE
                load = lambda j: halves[11 * half + j, pl.ds(parity, 192, stride=2), :]
                got = shifted(load, local - low, WIDE // TILE - 1)
                value = jnp.where(between_lanes(value.shape, low, high), got, value)
            out_ref[pl.ds(b, 192, stride=PAIR), :] = value

    for own_y in range(2):

        @pl.when((x == 1) & (d >= 5) & (y == own_y))
        def _(own_y=own_y):
            for q in range(4):
                half, part = q // 2, q % 2
                ref = block_refs[(1 - half) * 2 + (part ^ own_y)]

                @pl.when(d == 5)
                def _():
                    for j in range(8):
                        first = (6, 5)[part] * TILE + 176 * j
                        value = ref[first : first + 176, :].astype(f32)
                        out_ref[pl.ds(8 * (344 + 172 * q) + j, 176, stride=8), :] = value

                @pl.when(d > 5)
                def _():
                    for j in range(8):
                        value = ref[272 * j : 272 * j + 272, :].astype(f32)
                        out_ref[pl.ds(8 * 258 * q + j, 264, stride=8), :] = value[:264]


def flat_kernel(start_ref, lined_ref, left_ref, right_ref, out_ref, buf, staged, sem):
    buf[:8, :] = left_ref[...]
    buf[8 : 8 + LINED, :] = lined_ref[:LINED, :]
    buf[8 + LINED :, :] = jnp.zeros((buf.shape[0] - 8 - LINED, 128), f32)

    @pl.when(start_ref[1] == 0)
    def _():
        buf[8 + 8192 : 8 + 8192 + 256, :] = right_ref[...]

    staged[...] = buf[pl.ds(start_ref[0], SHARD), :]
    copy = pltpu.make_async_copy(staged, out_ref.reshape(SHARD, 128), sem)
    copy.start()
    copy.wait()


def padded(m, rows):
    return jnp.pad(m, ((0, rows - m.shape[0]), (0, 0)))


def dp_right(value):
    return lax.ppermute(value, AXES, [(8 * s + i, 8 * s + i + 1) for s in range(4) for i in range(7)])


def dp_left(value):
    return lax.ppermute(value, AXES, [(8 * s + i + 1, 8 * s + i) for s in range(4) for i in range(7)])


def source_blocks(flat_params, y, x, z, c, d):
    tail = flat_params[:, -LEFT * 128 :].reshape(LEFT, 128)
    head = flat_params[:, :1024].reshape(8, 128)
    left, right = dp_right(tail), dp_left(head)
    start = jnp.maximum(200 - jnp.where(x == 0, 65 * d, d), 0)
    blocks, moved = pl.pallas_call(
        source_kernel,
        in_specs=[
            pl.BlockSpec(memory_space=pltpu.SMEM),
            pl.BlockSpec(memory_space=pl.ANY),
            pl.BlockSpec(memory_space=pltpu.VMEM),
            pl.BlockSpec(memory_space=pltpu.VMEM),
        ],
        out_shape=[
            jax.ShapeDtypeStruct((4, ROWS + GAIN, TILE), bf16),
            jax.ShapeDtypeStruct((2, ROWS + GAIN, TILE), bf16),
        ],
        scratch_shapes=[pltpu.VMEM((8576, TILE), f32), pltpu.VMEM((384, TILE), f32), pltpu.SemaphoreType.DMA],
        compiler_params=pltpu.CompilerParams(vmem_limit_bytes=40 * 2**20),
    )(jnp.stack([start, x, y, d]), flat_params, left, right)
    moved = route(moved, lambda yy, xx, zz, cc: (0, 0, 1, 0) if (yy, xx, zz, cc) == (0, 0, 0, 1) else None)
    from_x, from_xy = swap_x(blocks[2]), swap_xy(blocks[3])
    swapped = (y == 0) & (x == 0) & (d == 2)
    own, flipped = jnp.where(swapped, moved[0], blocks[0]), jnp.where(swapped, moved[1], blocks[1])
    from_y = swap_y(flipped)
    own_units, own_rows = jnp.where(x == 0, own, from_x), jnp.where(x == 0, from_x, own)
    other_units, other_rows = jnp.where(x == 0, from_y, from_xy), jnp.where(x == 0, from_xy, from_y)
    size = UNIT + GAIN

    pick = lambda owner, own, other: jnp.where(y == owner, own, other)
    units = [pick(owner, own_units, other_units) for owner in (0, 1)]
    ahead = along_z(jnp.stack([unit[size : 2 * size] for unit in units]), {0: 2, 1: 3})
    units = [jnp.where(z < 2, unit[:size], later) for unit, later in zip(units, ahead)]
    rows = [pick(owner, own_rows, other_rows) for owner in (0, 1)]
    return jnp.concatenate([units[0], rows[0], units[1]], axis=0), rows[1]


def fetch(places, gathered_refs, blocks, sems):
    copies, done = [], 0
    for i, ((first, rows), ref) in enumerate(zip(places, gathered_refs)):
        for p in range(16):
            target = blocks.at[p, pl.ds(done, rows)]
            copies.append(pltpu.make_async_copy(ref.at[p, pl.ds(first, rows)], target, sems.at[16 * i + p]))
        done += rows
    for copy in copies:
        copy.start()
    return copies


def unit_weights_kernel(section, places, gathered_ref, _, *refs):
    *out_refs, gain_ref, blocks, wide, sems = refs
    for copy in fetch(places, [gathered_ref], blocks, sems):
        copy.wait()
    owner = section // 2
    gain_ref[...] = blocks[spot(owner, 0, 0), UNIT : UNIT + GAIN, :]
    q_ref, k_ref, v_ref, o_ref = out_refs
    for k in range(4):
        block = lambda d, low, high: blocks[spot(k % 2, d // 2 + 2 * (k // 2), d % 2), low:high, :]
        lanes = slice(128 * k, 128 * k + 128)
        far = slice(512 + 128 * k, 512 + 128 * k + 128)
        if section:
            q_ref[:, lanes] = block(0, 0, 1024)
            k_ref[:, lanes] = block(1, 0, 1024)
            v_ref[:, lanes] = block(2, 0, 1024)
            o_ref[:, lanes] = block(3, 0, 512)
            o_ref[:, far] = block(3, 512, 1024)
        else:
            wide[0, pl.ds(k, 256, stride=4), :] = block(0, 0, 256).astype(f32)
            wide[1, pl.ds(k, 256, stride=4), :] = block(0, 256, 512).astype(f32)
            v_ref[:512, lanes] = block(0, 512, 1024)
            v_ref[512:, lanes] = block(1, 0, 512)
            o_ref[:, lanes] = block(2, 0, 512)
            o_ref[:, far] = block(2, 512, 1024)
    if section == 0:
        q_ref[...] = wide[0].astype(bf16)
        k_ref[...] = wide[1].astype(bf16)


def unit_weights(section, earlier, places, *gathered):
    narrow = (D, 512 if section else 128)
    shapes = [narrow, narrow, (D, 512), (512, D), (GAIN, TILE)]
    *weights, gain = pl.pallas_call(
        partial(unit_weights_kernel, section, places),
        in_specs=[pl.BlockSpec(memory_space=pltpu.HBM), pl.BlockSpec(memory_space=pl.ANY)],
        out_shape=[jax.ShapeDtypeStruct(shape, bf16) for shape in shapes],
        scratch_shapes=[
            pltpu.VMEM((16, UNIT + GAIN, TILE), bf16),
            pltpu.VMEM((2, 1024, TILE), f32),
            pltpu.SemaphoreType.DMA((16,)),
        ],
        compiler_params=pltpu.CompilerParams(vmem_limit_bytes=40 * 2**20),
    )(*gathered, earlier)
    return gain[:8].reshape(1, D).astype(f32), tuple(weights)


def row_places():
    places = []
    for d in range(6):
        for part, count, skipped in ((0, 17 if d < 5 else 6, 0), (1, 16 if d < 5 else 5, 17 if d < 5 else 6)):
            places.append((spot(part, d // 2, d % 2), 33 * d + skipped, count))
    return places


def strip_places():
    places = [(spot(part, 2, 1), (6, 5)[part] * TILE, 176, 176 * part, 176) for part in (0, 1)]
    for i in range(4):
        places.append((spot(i % 2, 3, i // 2), 0, 272, 352 + 264 * i, 264))
    return places


def row_weights_kernel(section, places, *refs):
    gathered_refs = refs[: len(places)]
    gate_ref, up_ref, down_ref, gain_ref, blocks, wide, sems = refs[len(places) + 1 :]
    for copy in fetch(places, gathered_refs, blocks, sems):
        copy.wait()
    gain_ref[...] = blocks[spot(section // 2, 0, 0), ROWS : ROWS + GAIN, :]
    for p, start, count in row_places():
        for i in range(count):
            r, j = (start + i) // 11, (start + i) % 11
            ref = gate_ref if r < 8 else up_ref
            ref[TILE * (r % 8) : TILE * (r % 8) + TILE, TILE * j : TILE * j + TILE] = blocks[
                p, TILE * i : TILE * i + TILE, :
            ]
    for p, start, step, unit, count in strip_places():
        for j in range(8):
            value = blocks[p, start + step * j : start + step * j + step, :].astype(f32)
            wide[unit : unit + count, TILE * j : TILE * j + TILE] = value[:count]
    down_ref[...] = wide[...].astype(bf16)


def row_weights(section, earlier, places, *gathered):
    shapes = [(D, WIDE), (D, WIDE), (WIDE, D), (GAIN, TILE)]
    *weights, gain = pl.pallas_call(
        partial(row_weights_kernel, section, places),
        in_specs=[pl.BlockSpec(memory_space=pltpu.HBM)] * len(places) + [pl.BlockSpec(memory_space=pl.ANY)],
        out_shape=[jax.ShapeDtypeStruct(shape, bf16) for shape in shapes],
        scratch_shapes=[
            pltpu.VMEM((16, ROWS + GAIN, TILE), bf16),
            pltpu.VMEM((WIDE, D), f32),
            pltpu.SemaphoreType.DMA((16 * len(places),)),
        ],
        compiler_params=pltpu.CompilerParams(vmem_limit_bytes=48 * 2**20),
    )(*gathered, earlier)
    return gain[:8].reshape(1, D).astype(f32), tuple(weights)


def halves_of(refs):
    if len(refs) == 2:
        return refs
    rows = refs[0].shape[0] // 2
    return refs[0].at[:rows], refs[0].at[rows:]


def dot_rows(first, lanes, second):
    return sum(dot_tn(a[:, lanes], b[...]) for a, b in zip(first, second))


def grouped(counts, refs):
    groups, at = [], 0
    for count in counts:
        group = refs[at : at + count]
        groups.append(group if len(set(counts)) == 1 else halves_of(group))
        at += count
    return groups, refs[at:]


def pack_rows_kernel(counts, *refs):
    (hidden, gate, up, activ, grad), refs = grouped(counts, refs)
    _, out_ref, done_ref, wide = refs
    done_ref[...] = jnp.zeros_like(done_ref)
    place_of = {}
    for p, start, count in row_places():
        for i in range(count):
            place_of[start + i] = (p, i)
    for side, local in enumerate((gate, up)):
        for first in (0, 512):
            value = dot_rows(hidden, slice(first, first + 512), local).astype(bf16)
            for r in range(4):
                for j in range(11):
                    p, i = place_of[11 * (8 * side + first // TILE + r) + j]
                    out_ref[p, TILE * i : TILE * i + TILE, :] = value[
                        TILE * r : TILE * r + TILE, TILE * j : TILE * j + TILE
                    ]
    for first, count in ((0, 512), (512, 512), (1024, 384)):
        wide[first : first + count, :] = dot_rows(activ, slice(first, first + count), grad)
    wide[WIDE:, :] = jnp.zeros((8, D), f32)
    for p, start, step, unit, _ in strip_places():
        for j in range(8):
            value = wide[unit : unit + step, TILE * j : TILE * j + TILE].astype(bf16)
            out_ref[p, start + step * j : start + step * j + step, :] = value


def pack_rows(hidden, grad_gate, grad_up, activ, grad, earlier):
    operands = (hidden, grad_gate, grad_up, activ, grad)
    counts = [len(operand) for operand in operands]
    return pl.pallas_call(
        partial(pack_rows_kernel, counts),
        in_specs=[pl.BlockSpec(memory_space=pltpu.VMEM)] * sum(counts) + [pl.BlockSpec(memory_space=pl.ANY)],
        out_shape=[jax.ShapeDtypeStruct((16, ROWS, TILE), bf16), jax.ShapeDtypeStruct((8, TILE), f32)],
        scratch_shapes=[pltpu.VMEM((WIDE + 8, D), f32)],
        compiler_params=pltpu.CompilerParams(vmem_limit_bytes=48 * 2**20),
        cost_estimate=pl.CostEstimate(flops=2 * 512 * 3 * D * WIDE, bytes_accessed=2**24, transcendentals=0),
    )(*sum(map(list, operands), []), earlier)


def pack_units_kernel(section, counts, info_ref, *refs):
    y, z, c = info_ref[0], info_ref[1], info_ref[2]
    (hidden, grad, gq, gk, gv, mixed), refs = grouped(counts, refs)
    _, out_ref, done_ref, *scratch = refs
    done_ref[...] = jnp.zeros_like(done_ref)

    def store(d, k, low, high, value):
        base = UNIT * (k // 2)
        out_ref[c ^ (d % 2), y ^ (k % 2), (d // 2) ^ (z & 1), base + low : base + high, :] = value

    if section:
        for d, local in enumerate((gq, gk, gv)):
            for r in range(4):
                value = dot_rows(hidden, slice(256 * r, 256 * r + 256), local).astype(bf16)
                for k in range(4):
                    store(d, k, 256 * r, 256 * r + 256, value[:, 128 * k : 128 * k + 128])
        out_d = 3
    else:
        (wide,) = scratch
        for d, local in enumerate((gq, gk)):
            for r in range(4):
                wide[d, 256 * r : 256 * r + 256, :] = dot_rows(hidden, slice(256 * r, 256 * r + 256), local)
            for k in range(4):
                store(0, k, 256 * d, 256 * d + 256, wide[d, pl.ds(k, 256, stride=4), :].astype(bf16))
        for r in range(4):
            value = dot_rows(hidden, slice(256 * r, 256 * r + 256), gv).astype(bf16)
            for k in range(4):
                low = (512, 768, 0, 256)[r]
                store(0 if r < 2 else 1, k, low, low + 256, value[:, 128 * k : 128 * k + 128])
        for k in range(4):
            store(1, k, 512, 1024, jnp.zeros((512, TILE), bf16))
            store(3, k, 0, 1024, jnp.zeros((1024, TILE), bf16))
        out_d = 2
    for r in range(2):
        value = dot_rows(mixed, slice(256 * r, 256 * r + 256), grad).astype(bf16)
        for k in range(8):
            low = 512 * (k // 4) + 256 * r
            store(out_d, k % 4, low, low + 256, value[:, 128 * k : 128 * k + 128])


def pack_units(section, place, hidden, gq, gk, gv, mixed, grad, earlier):
    operands = (hidden, grad, [gq], [gk], [gv], [mixed])
    counts = [len(operand) for operand in operands]
    return pl.pallas_call(
        partial(pack_units_kernel, section, counts),
        in_specs=[pl.BlockSpec(memory_space=pltpu.SMEM)]
        + [pl.BlockSpec(memory_space=pltpu.VMEM)] * sum(counts)
        + [pl.BlockSpec(memory_space=pl.ANY)],
        out_shape=[jax.ShapeDtypeStruct((2, 2, 2, 2 * UNIT, TILE), bf16), jax.ShapeDtypeStruct((8, TILE), f32)],
        scratch_shapes=[] if section else [pltpu.VMEM((2, UNIT, TILE), f32)],
        compiler_params=pltpu.CompilerParams(vmem_limit_bytes=40 * 2**20),
        cost_estimate=pl.CostEstimate(flops=2 * 512 * 4 * D * 512, bytes_accessed=2**23, transcendentals=0),
    )(place, *sum(map(list, operands), []), earlier)


def add(first, second):
    return (first.astype(f32) + second.astype(f32)).astype(bf16)


def scattered(blocks):
    return lax.psum_scatter(blocks, GROUP, scatter_dimension=0, tiled=False)


def param_shard(units, rows, gain, place_rows, received, y, x, z, c, d):
    pick = lambda owner, pair: jnp.where(y == owner, pair[0], pair[1])
    units = [padded(unit, ROWS) for unit in units]
    own_units, other_units = pick(0, units), pick(1, units)
    own_rows, other_rows = pick(0, rows), pick(1, rows)
    from_x = swap_x(jnp.where(x == 0, own_rows, own_units))
    from_xy = swap_xy(jnp.where(x == 0, other_rows, other_units))
    from_y = swap_y(jnp.where(x == 0, other_units, other_rows))
    from_x, gain, *sent, got_out, got_grad = tied(from_x, gain, own_units, other_units, *received)
    results = place_rows((got_out, got_grad))
    gain = gain + along_z(gain, {0: 2, 2: 0, 1: 3, 3: 1})
    gain_own = lax.dynamic_index_in_dim(gain, 2 * y + x, 0, keepdims=True)
    own = jnp.where(x == 0, own_units, own_rows)
    moved = [
        route(block, lambda yy, xx, zz, cc: (0, 0, 0, 1) if (yy, xx, zz, cc) == (source, 0, 1, 0) else None)
        for source, block in enumerate(sent)
    ]
    lined = pl.pallas_call(
        line_kernel,
        in_specs=[pl.BlockSpec(memory_space=pltpu.SMEM)]
        + [pl.BlockSpec(memory_space=pltpu.VMEM)] * 6
        + [pl.BlockSpec(memory_space=pl.ANY)] * 2,
        out_shape=jax.ShapeDtypeStruct((LINED + 64, TILE), f32),
        scratch_shapes=[pltpu.VMEM((22, 384, TILE), f32)],
        compiler_params=pltpu.CompilerParams(vmem_limit_bytes=40 * 2**20),
    )(jnp.stack([x, y, d]), own, from_y, from_x, from_xy, *moved, *results)
    left = dp_right(jnp.where(x == 0, lined[8184:8192], lined[LINED - 8 : LINED]))
    right = dp_left(lined[:256])
    left = jnp.where(d == 0, gain_own.reshape(8, 128), left)
    start = jnp.where(x == 0, jnp.minimum(65 * d, 263), d)
    shard = pl.pallas_call(
        flat_kernel,
        in_specs=[pl.BlockSpec(memory_space=pltpu.SMEM)] + [pl.BlockSpec(memory_space=pltpu.VMEM)] * 3,
        out_specs=pl.BlockSpec(memory_space=pl.ANY),
        out_shape=jax.ShapeDtypeStruct((1, SHARD * 128), f32),
        scratch_shapes=[pltpu.VMEM((8528, 128), f32), pltpu.VMEM((SHARD, 128), f32), pltpu.SemaphoreType.DMA],
        compiler_params=pltpu.CompilerParams(vmem_limit_bytes=40 * 2**20),
    )(jnp.stack([start, x]), lined, left, right)
    return results, shard, gain_own


def mlp_grad(weights, kept, grad):
    w_gate, w_up, w_down = weights
    gate, up = kept[3:5]
    grad_activ = dot_right(grad, w_down)
    sig = jax.nn.sigmoid(gate)
    grad_gate = (grad_activ * up * sig * (1.0 + gate * (1.0 - sig))).astype(bf16)
    grad_up = (grad_activ * gate * sig).astype(bf16)
    partial_hidden = dot_right(grad_gate, w_gate) + dot_right(grad_up, w_up)
    return partial_hidden.astype(bf16), (grad_gate, grad_up)


def added(entry, *parts):
    return (entry.astype(f32) + sum(part.astype(f32) for part in parts)).astype(bf16)


def per_row(inputs, cotangent, seq_lengths, flat_params):
    y, x, z, c = (lax.axis_index(axis) for axis in AXES)
    d = 2 * z + c
    seg_ids = segment_ids(lax.dynamic_index_in_dim(seq_lengths, y, 0, keepdims=False)[0], inputs.shape[1])
    block0, block1 = source_blocks(flat_params, y, x, z, c, d)
    first = lax.all_gather(block0, GROUP)
    first, block1 = tied(first, block1)
    second = lax.all_gather(block1, GROUP)
    unit, rows = UNIT + GAIN, ROWS + GAIN
    gathered = [([(0, unit)], first), ([(unit, rows)], first), ([(unit + rows, unit)], first), ([(0, rows)], second)]
    gains, weights, kept, outputs = [None] * 4, [None] * 4, [None] * 4, [None] * 4
    row_half = inputs.shape[1] // 2

    def cut(rows):
        return [rows[:row_half], rows[row_half:]]

    def join(halves):
        return jnp.concatenate(halves, axis=0)

    def open_section(s, earlier):
        gains[s], weights[s] = (unit_weights if s % 2 == 0 else row_weights)(s, earlier, *gathered[s])
        kept[s] = []
        return gains[s]

    def normed_rows(s, entry):
        hidden, normed, inv_root = norm_forward(entry.astype(f32), gains[s])
        kept[s].append((hidden.astype(bf16), normed, inv_root))
        return kept[s][-1][0]

    def heads(s, entry):
        hidden = normed_rows(s, entry)
        return [dot_plain(hidden, w).astype(bf16) for w in weights[s][:3]]

    def attention(s, parts):
        q, k, v = (join(halves) for halves in zip(*parts))
        mixed = mix(s == 0, seg_ids, q, k, v)
        kept[s].append((q, k, v, mixed))
        return [dot_plain(half, weights[s][3]).astype(bf16) for half in cut(mixed)]

    def mlp(s, entry):
        hidden = normed_rows(s, entry)
        w_gate, w_up, _ = weights[s]
        gate = dot_plain(hidden, w_gate)
        up = dot_plain(hidden, w_up)
        activ = (jax.nn.silu(gate) * up).astype(bf16)
        kept[s][-1] += (gate, up, activ)
        return activ

    entry = cut(lax.dynamic_index_in_dim(inputs, y, 0, keepdims=False))
    open_section(0, entry[0])
    branch = attention(0, [heads(0, half) for half in entry])
    got = [swap_x(half) for half in branch]
    open_section(1, branch[0])
    entry[0] = added(entry[0], branch[0], got[0])
    next_branch = [dot_plain(mlp(1, entry[0]), weights[1][2]).astype(bf16)]
    got[1], next_branch[0] = tied(got[1], next_branch[0])
    entry[1] = added(entry[1], branch[1], got[1])
    outputs[0] = list(entry)
    next_branch.append(dot_plain(mlp(1, entry[1]), weights[1][2]).astype(bf16))
    branch = next_branch
    got = [swap_x(half) for half in branch]
    open_section(2, branch[1])
    entry[0] = added(entry[0], branch[0], got[0])
    first_heads = heads(2, entry[0])
    got[1], first_heads[0] = tied(got[1], first_heads[0])
    entry[1] = added(entry[1], branch[1], got[1])
    outputs[1] = list(entry)
    branch = join(attention(2, [first_heads, heads(2, entry[1])]))
    got = swap_x(branch)
    done = open_section(3, branch)
    got, _ = tied(got, done)

    grads, gain_sums, sums = [None] * 4, [0.0] * 4, [None] * 4
    place = jnp.stack([y, z, c])

    def finish(s, half, grad, part, got):
        grad_hidden = part.astype(f32) + got.astype(f32)
        _, normed, inv_root = kept[s][half][:3]
        grad_entry, grad_gain = norm_backward(grad_hidden, gains[s], normed, inv_root)
        gain_sums[s] += grad_gain
        return (grad.astype(f32) + grad_entry).astype(bf16)

    def finish_rows(s, grad, parts, got):
        return [finish(s, half, *rows) for half, rows in enumerate(zip(grad, parts, cut(got)))]

    def pack_mlp(s, local, grad, earlier):
        hidden = [half[0] for half in kept[s]]
        activ = [half[5] for half in kept[s]]
        return pack_rows(hidden, *([half[i] for half in local] for i in (0, 1)), activ, grad, earlier)

    def mix_parts(s, grad_mixed):
        q, k, v, mixed = kept[s][2]
        local = mix_grad(s == 0, seg_ids, q, k, v, join(grad_mixed))
        w_query, w_key, w_value, _ = weights[s]
        parts = []
        for gq, gk, gv in zip(*(cut(part) for part in local)):
            parts.append((dot_right(gq, w_query) + dot_right(gk, w_key) + dot_right(gv, w_value)).astype(bf16))
        return parts, local

    def pack_attention(s, local, grad, earlier):
        hidden = [half[0] for half in kept[s][:2]]
        return pack_units(s, place, hidden, *local, kept[s][2][3], grad, earlier)

    def near(value):
        return along_z(value, {0: 1, 1: 0, 2: 3, 3: 2})

    def far(value):
        return along_z(value, {2: 0, 3: 1})

    grad = lax.dynamic_index_in_dim(cotangent, y, 0, keepdims=False)
    entry = added(join(entry), branch, got)
    outputs[2] = [entry]
    branch = dot_plain(mlp(3, entry), weights[3][2]).astype(bf16)
    part, local = mlp_grad(weights[3], kept[3][0], grad)
    got = swap_x(part)
    packed, done = pack_mlp(3, [local], [grad], part)
    sums[3] = scattered(packed)
    got, _, branch = tied(got, done, branch)
    grad = finish(3, 0, grad, part, got)
    grads[3] = [grad]

    parts, local = mix_parts(2, [dot_right(grad, weights[2][3]).astype(bf16)])
    part, got_out = tied(join(parts), swap_x(branch))
    outputs[3] = [added(entry, branch, got_out)]
    got = swap_x(part)
    packed, done = pack_attention(2, local, [grad], part)
    got, _ = tied(got, done)
    grad = grads[2] = finish_rows(2, cut(grad), cut(part), got)
    parts2 = add(packed[0], swap_c(packed[1]))

    parts, local = zip(*(mlp_grad(weights[1], kept[1][half], grad[half]) for half in range(2)))
    part = join(parts)
    got = swap_x(part)
    packed, done = pack_mlp(1, local, grad, part)
    sums[1] = scattered(packed)
    got, _, got_y = tied(got, done, swap_y(parts2[1]))
    grad = grads[1] = finish_rows(1, grad, cut(part), got)
    parts2 = add(parts2[0], got_y)

    parts, local = mix_parts(0, [dot_right(half, weights[0][3]).astype(bf16) for half in grad])
    part = join(parts)
    got = swap_x(part)
    packed, _ = pack_attention(0, local, grad, part)
    parts0 = add(packed[0], swap_c(packed[1]))
    outputs = [join(halves) for halves in outputs]
    sent = by_index(2 * (1 - y) + x, outputs)
    got, got_y, got_z, sent = tied(got, swap_y(parts0[1]), near(parts2[1]), sent)
    parts0, parts2 = add(parts0[0], got_y), add(parts2[0], got_z)
    grads[0] = finish_rows(0, grad, cut(part), got)
    grads = [join(halves) for halves in grads]

    got_z, got_far = near(parts0[1]), far(parts2)
    gain = jnp.concatenate(gain_sums, axis=0)
    gain = gain + swap_c(gain)
    got_gain, sent, grad_sent = tied(swap_y(gain), sent, by_index(2 * (1 - y) + x, grads))
    got_out, got_grad = swap_y(sent), swap_y(grad_sent)
    gain, parts0 = gain + got_gain, add(parts0[0], got_z)
    gain, sums[0], sums[2] = gain + near(gain), add(parts0, far(parts0)), add(parts2, got_far)

    def place_rows(received):
        placed = []
        for rows_of, got in zip((outputs, grads), received):
            own = by_index(2 * y + x, rows_of)
            placed.append(jnp.stack([jnp.where(y == 0, own, got), jnp.where(y == 0, got, own)])[None])
        return placed

    results, shard, gain_own = param_shard(
        (sums[0], sums[2]), (sums[1], sums[3]), gain, place_rows, (got_out, got_grad), y, x, z, c, d
    )
    return *results, shard, gain_own


def solution(mesh):
    if mesh.shape["section"] == 4 and mesh.shape["dp"] == 2 * DEPTH:
        grid = jax.sharding.Mesh(mesh.devices.reshape(2, 2, DEPTH, 2), AXES)
        function, section, dp = per_row, ("y", "x"), ("z", "c")
    else:
        grid, function, section, dp = mesh, per_device, "section", "dp"
    return jax.shard_map(
        function,
        mesh=grid,
        in_specs=(P(None, dp, None), P(None, dp, None), P(None, dp, None), P(section, dp)),
        out_specs=(P(section, None, dp, None), P(section, None, dp, None), P(section, dp), P(section, None)),
        check_vma=False,
    )
```
